32 devices in a mesh: pos: 16 (over z, y, x), mode: 2 (over core).
Axes of the slice: x: 2, y: 2, z: 4, core: 2. Of those that a mesh axis runs over, the one named last changes fastest.
Arguments:
- object_field: float32 [2, 2048, 512], P(None, 'pos'), may hold values from -6 to 6
- probe: float32 [2, 8, 256, 256], P(None, 'mode'), may hold values from -3 to 3
- measured: float32 [48, 256, 256], P('pos'), may hold values from 0 to 16
- row_offsets: int32 [48], P('pos'), may hold values from 0 to 127
- col_offsets: int32 [48], P('pos'), may hold values from 0 to 256
- tile_counts: int32 [16], P('pos'), may hold values from 1 to 3, 24 in all
Outputs:
- updated_object: float32 [2, 2048, 512], P(None, ('pos', 'mode'))
The draws below stay inside these ranges and needn't reach their ends.
Inputs may be any that keep to these rules, and one draw needn't show every extreme that they name: Slots 0 to tile_counts[t] - 1 of tile t hold scan positions, the others are empty; the counts sum to 24 and the largest equals 3.
All inputs are finite; a program needn't handle non-finite values. No bound on the sum of `tile_counts` on one device may be relied on, other than what follows from the above.
Results may differ from the reference program's by a relative error of at most 0.0016.
Values sent between devices are 32-bit elements; how exact they have to be, the bound alone decides.
A program may use at most 64 MiB of HBM per device.

```python
import math
import jax
import jax.numpy as jnp
import numpy as np
from jax import lax

PAT = 256
MODES = 8
TILE_H = 128
OBJ_W = 512
SLOTS = 3
TILES = 16
OBJ_H = 2048
POSITIONS = 48
LIVE = 24


def set_ends(entries, stream_key, low, high):
    longest = entries.shape.index(max(entries.shape))
    spots = []
    for shift in (0, 1):
        where = [jax.random.randint(jax.random.fold_in(stream_key, axis), (), 0, length) for axis, length in enumerate(entries.shape)]
        where[longest] = (where[longest] + shift) % entries.shape[longest]
        spots.append(tuple(where))
    return entries.at[spots[0]].set(low).at[spots[1]].set(high)


def block_scale(own_key, shape, pieces, low, high):
    loudness, own = 1.0, jax.random.fold_in(own_key, 6)
    for dim, blocks in pieces:
        heights = jnp.exp(jax.random.uniform(jax.random.fold_in(own, dim), (blocks,), jnp.float32, low / len(pieces), high / len(pieces)))
        loudness = loudness * jnp.repeat(heights, shape[dim] // blocks).reshape([-1 if axis == dim else 1 for axis in range(len(shape))])
    return loudness


def split_up(amount, total, limit, lean):
    weights = [(1 << 20) // math.isqrt(rank ** lean) + 1 for rank in range(2, amount + 1)]
    spare, given = total - limit - (amount - 1), [1] * (amount - 1)
    while spare > 0:
        candidates = [i for i in range(amount - 1) if given[i] < limit]
        mass, left = sum([weights[i] for i in candidates]), spare
        for i in candidates:
            more = min(limit - given[i], max(1, left * weights[i] // mass), spare)
            given[i] = given[i] + more
            spare = spare - more
    return np.array([limit] + given)


def ragged_sizes(key, count, total, limit, lean):
    if count == 2:
        one = jax.random.randint(key, (), max(1, total - limit), min(limit, total - 1) + 1)
        return jnp.stack([one, total - one])
    tallies = jnp.asarray(split_up(count, total, limit, lean), jnp.int32)
    twos = (count - 1) // 2
    giver, taker = tallies[1:1 + 2 * twos:2], tallies[2:2 + 2 * twos:2]
    slack = jnp.minimum(giver - 1, limit - taker)
    passed = jax.random.randint(jax.random.fold_in(key, 1), (twos,), 0, 1 << 20) % (slack + 1)
    tallies = tallies.at[1:1 + 2 * twos:2].set(giver - passed).at[2:2 + 2 * twos:2].set(taker + passed)
    return tallies[jax.random.permutation(jax.random.fold_in(key, 2), count)]


def noise(stream_key, extent, width, limit, shards=(), kind=jnp.bfloat16):
    factor_of = block_scale(stream_key, extent, shards, -0.22, 0.18) if shards else 1.0
    values = jax.random.normal(stream_key, extent, jnp.float32) * width * factor_of
    return jnp.minimum(jnp.maximum(values, -limit), limit).astype(kind)


def setup_inputs(seed: int = 0) -> dict:
    seeds = jax.random.split(jax.random.key(seed), 7)
    return {
        "object_field": noise(seeds[0], (2, OBJ_H, OBJ_W), 1.0, 6.0, ((1, 16),), jnp.float32),
        "probe": noise(seeds[1], (2, MODES, PAT, PAT), 0.5, 3.0, ((1, 2),), jnp.float32),
        "measured": jnp.clip(16.0 * jax.random.uniform(seeds[2], (POSITIONS, PAT, PAT), jnp.float32) ** block_scale(seeds[2], (POSITIONS, PAT, PAT), ((0, 16),), -0.2, 0.2), 0.0, 16.0),
        "row_offsets": set_ends(jax.random.randint(seeds[3], (POSITIONS,), 0, TILE_H), jax.random.fold_in(seeds[3], 1), 0, TILE_H - 1).astype(jnp.int32),
        "col_offsets": set_ends(jax.random.randint(seeds[4], (POSITIONS,), 0, OBJ_W - PAT + 1), jax.random.fold_in(seeds[4], 1), 0, OBJ_W - PAT).astype(jnp.int32),
        "tile_counts": ragged_sizes(seeds[5], TILES, LIVE, SLOTS, 2).astype(jnp.int32),
    }


def dft_tables(pattern):
    counter = jnp.arange(pattern, dtype=jnp.int32)
    phases = counter[:, None] * counter[None, :] % pattern
    angles = phases.astype(jnp.float32) * (2.0 * math.pi / pattern)
    factor = 1.0 / math.sqrt(pattern)
    return ((jnp.cos(angles) * factor).astype(jnp.bfloat16), (-jnp.sin(angles) * factor).astype(jnp.bfloat16))

def reference(object_field, probe, measured, row_offsets, col_offsets, tile_counts):
    real_table, imag_table = dft_tables(PAT)
    real_wide = real_table.astype(jnp.float32)
    imag_wide = imag_table.astype(jnp.float32)
    padded = jnp.pad(object_field, ((0, 0), (TILE_H, TILE_H), (0, 0)))
    probe_re = probe[0]
    probe_im = probe[1]
    probe_power = lax.optimization_barrier(jnp.sum(probe_re * probe_re + probe_im * probe_im, axis=0))
    anchor = jnp.zeros((), jnp.int32)

    def one_position(position, buffer):
        position = jnp.asarray(position).astype(jnp.int32)
        tile_id = position // SLOTS
        is_live = position % SLOTS < tile_counts[tile_id].astype(jnp.int32)
        top_row = (tile_id * TILE_H + TILE_H + row_offsets[position].astype(jnp.int32) - PAT // 2).astype(jnp.int32)
        column = col_offsets[position].astype(jnp.int32)
        window = lax.dynamic_slice(padded, (anchor, top_row, column), (2, PAT, PAT))
        exit_re = (probe_re * window[0] - probe_im * window[1]).astype(jnp.bfloat16)
        exit_im = (probe_re * window[1] + probe_im * window[0]).astype(jnp.bfloat16)
        wide_re = exit_re.astype(jnp.float32)
        wide_im = exit_im.astype(jnp.float32)
        half_re = (jnp.einsum('ua,kab->kub', real_wide, wide_re) - jnp.einsum('ua,kab->kub', imag_wide, wide_im)).astype(jnp.bfloat16).astype(jnp.float32)
        half_im = (jnp.einsum('ua,kab->kub', real_wide, wide_im) + jnp.einsum('ua,kab->kub', imag_wide, wide_re)).astype(jnp.bfloat16).astype(jnp.float32)
        wave_re = jnp.einsum('kub,bv->kuv', half_re, real_wide) - jnp.einsum('kub,bv->kuv', half_im, imag_wide)
        wave_im = jnp.einsum('kub,bv->kuv', half_re, imag_wide) + jnp.einsum('kub,bv->kuv', half_im, real_wide)
        model_power = lax.optimization_barrier(jnp.sum(wave_re * wave_re + wave_im * wave_im, axis=0))
        scaling = jnp.sqrt(measured[position]) / jnp.maximum(jnp.sqrt(model_power), 1.0)
        fixed_re = (scaling * wave_re).astype(jnp.bfloat16).astype(jnp.float32)
        fixed_im = (scaling * wave_im).astype(jnp.bfloat16).astype(jnp.float32)
        back_re = (jnp.einsum('ua,kab->kub', real_wide, fixed_re) + jnp.einsum('ua,kab->kub', imag_wide, fixed_im)).astype(jnp.bfloat16).astype(jnp.float32)
        back_im = (jnp.einsum('ua,kab->kub', real_wide, fixed_im) - jnp.einsum('ua,kab->kub', imag_wide, fixed_re)).astype(jnp.bfloat16).astype(jnp.float32)
        delta_re = jnp.einsum('kub,bv->kuv', back_re, real_wide) + jnp.einsum('kub,bv->kuv', back_im, imag_wide) - wide_re
        delta_im = jnp.einsum('kub,bv->kuv', back_im, real_wide) - jnp.einsum('kub,bv->kuv', back_re, imag_wide) - wide_im
        numer_re = lax.optimization_barrier(jnp.sum(probe_re * delta_re + probe_im * delta_im, axis=0))
        numer_im = lax.optimization_barrier(jnp.sum(probe_re * delta_im - probe_im * delta_re, axis=0))
        contrib = jnp.stack([numer_re, numer_im, probe_power])
        contrib = jnp.where(is_live, contrib, jnp.zeros_like(contrib))
        corner = (anchor, top_row, column)
        current = lax.dynamic_slice(buffer, corner, (3, PAT, PAT))
        return lax.dynamic_update_slice(buffer, current + contrib, corner)
    buffer = jnp.zeros((3, OBJ_H + 2 * TILE_H, OBJ_W), jnp.float32)
    buffer = lax.fori_loop(0, POSITIONS, one_position, buffer)
    inner = buffer[:, TILE_H:TILE_H + OBJ_H]
    return object_field + inner[:2] / (inner[2] + 1.0)
```

```python
import functools
import math

import jax
import jax.numpy as jnp
import numpy as np
from jax import lax
from jax.experimental import pallas as pl
from jax.experimental.pallas import tpu as pltpu
from jax.sharding import PartitionSpec as P

MESH = pl.DeviceIdType.MESH


def dft_tables(pattern):
    counter = np.arange(pattern)
    angles = (counter[:, None] * counter[None, :] % pattern) * (2.0 * math.pi / pattern)
    factor = 1.0 / math.sqrt(pattern)
    real = (np.cos(angles) * factor).astype(np.float32)
    imag = (-np.sin(angles) * factor).astype(np.float32)
    plain = np.block([[real, -imag], [imag, real]]).astype(jnp.bfloat16)
    turned = np.block([[real, imag], [-imag, real]]).astype(jnp.bfloat16)
    return plain, turned


def kernel(
    n, nm, chunks,
    row_ref, col_ref, count_ref, obj_ref, probe_ref, meas_ref, plain_ref, turned_ref,
    out_ref,
    ext, acc, illum, exit_ref, wave_ref, power, power_in, pp, pp_in, red_in,
    far_out, far_in, near_out, near_in, il_far_in, il_near_out, il_near_in,
    halo_s, halo_r, fwd_s, fwd_r, brn_s, brn_r, brf_s, brf_r,
    pow_s, pow_r, pp_s, pp_r, ilf_s, ilf_r, iln_s, iln_r,
    red_s, red_r, rf_s, rf_r, rn_s, rn_r,
):
    tile, cols = obj_ref.shape[1], obj_ref.shape[2]
    slots, pat = meas_ref.shape[0], meas_ref.shape[1]
    modes = probe_ref.shape[1]
    share = tile // nm
    piece = share // chunks
    lift = tile - pat // 2

    p = lax.axis_index("pos")
    m = lax.axis_index("mode")
    odd = lax.rem(p, 2)
    near_dev = p + 1 - 2 * odd
    far_blk = 2 * odd
    near_blk = 2 - far_blk
    far_raw = p - 2 + 4 * odd
    back_raw = p + 2 - 4 * odd
    has_far = jnp.logical_and(far_raw >= 0, far_raw < n)
    has_back = jnp.logical_and(back_raw >= 0, back_raw < n)
    far_dev = lax.rem(far_raw + n, n)
    back_dev = lax.rem(back_raw + n, n)
    others = [lax.rem(m + j, nm) for j in range(1, nm)]

    def rows_of(block, mode, c=0, size=None):
        size = share if size is None else size
        return pl.ds(pl.multiple_of(block * tile + mode * share + c * piece, 8), size)

    def remote(src, dst, s, r, pos, mode):
        return pltpu.make_async_remote_copy(
            src_ref=src, dst_ref=dst, send_sem=s, recv_sem=r,
            device_id=(pos, mode), device_id_type=MESH,
        )

    barrier = pltpu.get_barrier_semaphore()
    pl.semaphore_signal(barrier, inc=1, device_id=(near_dev, m), device_id_type=MESH)
    for other in others:
        pl.semaphore_signal(barrier, inc=1, device_id=(p, other), device_id_type=MESH)

    @pl.when(has_far)
    def _():
        pl.semaphore_signal(barrier, inc=1, device_id=(far_dev, m), device_id_type=MESH)

    @pl.when(has_back)
    def _():
        pl.semaphore_signal(barrier, inc=1, device_id=(back_dev, m), device_id_type=MESH)

    greeted = has_far.astype(jnp.int32) + has_back.astype(jnp.int32)
    pl.semaphore_wait(barrier, nm + greeted)

    def halo(c):
        return remote(
            obj_ref.at[:, rows_of(0, m, c, piece), :], ext.at[:, rows_of(far_blk, m, c, piece), :],
            halo_s.at[c], halo_r.at[c], near_dev, m,
        )

    def forward_near(c):
        return remote(
            ext.at[:, rows_of(near_blk, m, c, piece), :],
            ext.at[:, rows_of(far_blk, m, c, piece), :],
            fwd_s.at[c], fwd_r.at[c], back_dev, m,
        )

    def spread(block, c, j, s, r):
        where = rows_of(block, m, c, piece)
        return remote(
            ext.at[:, where, :], ext.at[:, where, :], s.at[j, c], r.at[j, c], p, others[j]
        )

    for c in range(chunks):
        halo(c).start()

    total = jnp.zeros((pat, pat), jnp.float32)
    for k in range(modes):
        total = total + probe_ref[0, k] * probe_ref[0, k] + probe_ref[1, k] * probe_ref[1, k]
    pp[...] = total

    def pp_copy(j):
        return remote(pp, pp_in.at[j], pp_s.at[j], pp_r.at[j], p, others[j])

    for j in range(nm - 1):
        pp_copy(j).start()

    ext[:, tile : 2 * tile, :] = obj_ref[...]
    acc[...] = jnp.zeros_like(acc)
    illum[...] = jnp.zeros_like(illum)

    @pl.when(jnp.logical_not(has_far))
    def _():
        ext[:, pl.ds(pl.multiple_of(far_blk * tile, 8), tile), :] = jnp.zeros(
            (2, tile, cols), jnp.float32
        )

    for c in range(chunks):
        halo(c).wait_recv()

        @pl.when(has_back)
        def _():
            forward_near(c).start()

        for j in range(nm - 1):
            spread(near_blk, c, j, brn_s, brn_r).start()

    for j in range(nm - 1):
        pp_copy(j).wait_recv()

    live = count_ref[0]

    steps = []
    while sum(steps) < (3 * tile - pat) // 8 - 1:
        steps.insert(0, max(1, 2 * sum(steps[:1])))

    def placed(values, slot):
        top = lift + row_ref[slot]
        by = lax.rem(top, 8)
        groups = lax.div(top, 8)
        turned_rows = pltpu.roll(values.reshape(pat // 8, 8, pat), by, 1)
        blank = jnp.zeros((1, 8, pat), jnp.float32)
        upper = jnp.concatenate([turned_rows, blank], axis=0)
        lower = jnp.concatenate([blank, turned_rows], axis=0)
        line = lax.broadcasted_iota(jnp.int32, (1, 8, pat), 1)
        values = jnp.where(line >= by, upper, lower).reshape(pat + 8, pat)
        wide = jnp.concatenate([values, jnp.zeros((pat + 8, cols - pat), jnp.float32)], axis=1)
        wide = pltpu.roll(wide, col_ref[slot], 1).reshape(pat // 8 + 1, 8, cols)
        for step in reversed(steps):
            blank = jnp.zeros((step, 8, cols), jnp.float32)
            far = lax.rem(lax.div(groups, step), 2) == 1
            wide = jnp.where(
                far,
                jnp.concatenate([blank, wide], axis=0),
                jnp.concatenate([wide, blank], axis=0),
            )
        return wide.reshape(3 * tile, cols)

    def window(part, slot):
        top = lift + row_ref[slot]
        by = lax.rem(top, 8)
        groups = lax.div(top, 8)
        rows = ext[part].reshape(3 * tile // 8, 8, cols)
        for step in steps:
            far = lax.rem(lax.div(groups, step), 2) == 1
            rows = jnp.where(far, rows[step:], rows[:-step])
        turn = lax.rem(cols - col_ref[slot], cols)
        rows = pltpu.roll(rows.reshape(pat + 8, cols), turn, 1)
        rows = rows[:, :pat].reshape(pat // 8 + 1, 8, pat)
        rows = pltpu.roll(rows, lax.rem(8 - by, 8), 1)
        line = lax.broadcasted_iota(jnp.int32, (1, 8, pat), 1)
        return jnp.where(line < 8 - by, rows[:-1], rows[1:]).reshape(pat, pat)

    def add_illum(s, carry):
        whole = pp[...]
        for j in range(nm - 1):
            whole = whole + pp_in[j]
        whole = jnp.where(s < live, whole, 0.0)
        illum[...] += placed(whole, s)
        return carry

    lax.fori_loop(0, slots, add_illum, 0)

    @pl.when(has_far)
    def _():
        for c in range(chunks):
            forward_near(c).wait_recv()
            for j in range(nm - 1):
                spread(far_blk, c, j, brf_s, brf_r).start()

    def illum_far():
        return remote(
            illum.at[rows_of(far_blk, m), :], il_far_in, ilf_s.at[0], ilf_r.at[0], far_dev, m
        )

    def illum_near():
        return remote(il_near_out, il_near_in, iln_s.at[0], iln_r.at[0], near_dev, m)

    @pl.when(has_far)
    def _():
        illum_far().start()

    for c in range(chunks):
        for j in range(nm - 1):
            spread(near_blk, c, j, brn_s, brn_r).wait_recv()

    @pl.when(has_far)
    def _():
        for c in range(chunks):
            for j in range(nm - 1):
                spread(far_blk, c, j, brf_s, brf_r).wait_recv()

    def power_copy(s, j):
        return remote(
            power.at[s], power_in.at[s, j], pow_s.at[s, j], pow_r.at[s, j], p, others[j]
        )

    def forward(s, carry):
        win_re = window(0, s)
        win_im = window(1, s)
        model = jnp.zeros((pat, pat), jnp.float32)
        for k in range(modes):
            probe_re, probe_im = probe_ref[0, k], probe_ref[1, k]
            exit_re = (probe_re * win_re - probe_im * win_im).astype(jnp.bfloat16)
            exit_im = (probe_re * win_im + probe_im * win_re).astype(jnp.bfloat16)
            stacked = jnp.concatenate([exit_re, exit_im], axis=0)
            exit_ref[s, k] = stacked
            half = jnp.dot(plain_ref[...], stacked, preferred_element_type=jnp.float32)
            half = half.astype(jnp.bfloat16)
            half = jnp.concatenate([half[:pat], half[pat:]], axis=1)
            wave = jnp.dot(half, turned_ref[...], preferred_element_type=jnp.float32)
            wave_ref[s, k] = wave
            model = model + wave[:, :pat] * wave[:, :pat] + wave[:, pat:] * wave[:, pat:]
        power[s] = model
        for j in range(nm - 1):
            power_copy(s, j).start()
        return carry

    lax.fori_loop(0, slots, forward, 0)

    @pl.when(has_back)
    def _():
        illum_far().wait_recv()
        il_near_out[...] = illum[rows_of(near_blk, m), :] + il_far_in[...]

    @pl.when(jnp.logical_not(has_back))
    def _():
        il_near_out[...] = illum[rows_of(near_blk, m), :]

    illum_near().start()

    def backward(s, carry):
        model = power[s]
        for j in range(nm - 1):
            power_copy(s, j).wait_recv()
            model = model + power_in[s, j]
        scaling = jnp.sqrt(meas_ref[s]) / jnp.maximum(jnp.sqrt(model), 1.0)
        numer_re = jnp.zeros((pat, pat), jnp.float32)
        numer_im = jnp.zeros((pat, pat), jnp.float32)
        for k in range(modes):
            fixed_re = (scaling * wave_ref[s, k, :, :pat]).astype(jnp.bfloat16)
            fixed_im = (scaling * wave_ref[s, k, :, pat:]).astype(jnp.bfloat16)
            fixed = jnp.concatenate([fixed_re, fixed_im], axis=0)
            back = jnp.dot(turned_ref[...], fixed, preferred_element_type=jnp.float32)
            back = back.astype(jnp.bfloat16)
            back = jnp.concatenate([back[:pat], back[pat:]], axis=1)
            delta = jnp.dot(back, plain_ref[...], preferred_element_type=jnp.float32)
            delta_re = delta[:, :pat] - exit_ref[s, k, :pat, :].astype(jnp.float32)
            delta_im = delta[:, pat:] - exit_ref[s, k, pat:, :].astype(jnp.float32)
            probe_re, probe_im = probe_ref[0, k], probe_ref[1, k]
            numer_re = numer_re + probe_re * delta_re + probe_im * delta_im
            numer_im = numer_im + probe_re * delta_im - probe_im * delta_re
        on = s < live
        acc[0] += placed(jnp.where(on, numer_re, 0.0), s)
        acc[1] += placed(jnp.where(on, numer_im, 0.0), s)
        return carry

    lax.fori_loop(0, slots, backward, 0)

    blocks = (far_blk, near_blk, 1)

    def reduce_copy(b, j):
        return remote(
            acc.at[:, rows_of(blocks[b], others[j]), :], red_in.at[j, b],
            red_s.at[j, b], red_r.at[j, b], p, others[j],
        )

    for b in range(3):
        for j in range(nm - 1):
            reduce_copy(b, j).start()

    def reduced(b):
        value = acc[:, rows_of(blocks[b], m), :]
        for j in range(nm - 1):
            reduce_copy(b, j).wait_recv()
            value = value + red_in[j, b]
        return value

    def far_copy(c):
        part = pl.ds(c * piece, piece)
        return remote(
            far_out.at[:, part, :], far_in.at[:, part, :], rf_s.at[c], rf_r.at[c], far_dev, m
        )

    def near_copy(c):
        part = pl.ds(c * piece, piece)
        return remote(
            near_out.at[:, part, :], near_in.at[:, part, :], rn_s.at[c], rn_r.at[c], near_dev, m
        )

    far_out[...] = reduced(0)

    @pl.when(has_far)
    def _():
        for c in range(chunks):
            far_copy(c).start()

    near_out[...] = reduced(1)
    for c in range(chunks):

        @pl.when(has_back)
        def _():
            part = pl.ds(c * piece, piece)
            far_copy(c).wait_recv()
            near_out[:, part, :] = near_out[:, part, :] + far_in[:, part, :]

        near_copy(c).start()

    own_sum = reduced(2)
    illum_near().wait_recv()
    weight = 1.0 / (illum[rows_of(1, m), :] + il_near_in[...] + 1.0)
    for c in range(chunks):
        near_copy(c).wait_recv()
        part = slice(c * piece, (c + 1) * piece)
        out_ref[:, part, :] = obj_ref[:, rows_of(0, m, c, piece), :] + (
            own_sum[:, part] + near_in[:, part, :]
        ) * weight[part]

    for c in range(chunks):
        halo(c).wait_send()
        near_copy(c).wait_send()
        for j in range(nm - 1):
            spread(near_blk, c, j, brn_s, brn_r).wait_send()
    for j in range(nm - 1):
        pp_copy(j).wait_send()
        for s in range(slots):
            power_copy(s, j).wait_send()
        for b in range(3):
            reduce_copy(b, j).wait_send()
    illum_near().wait_send()

    @pl.when(has_far)
    def _():
        illum_far().wait_send()
        for c in range(chunks):
            far_copy(c).wait_send()
            for j in range(nm - 1):
                spread(far_blk, c, j, brf_s, brf_r).wait_send()

    @pl.when(has_back)
    def _():
        for c in range(chunks):
            forward_near(c).wait_send()


def local(object_field, probe, measured, row_offsets, col_offsets, tile_counts):
    n, nm = lax.axis_size("pos"), lax.axis_size("mode")
    tile, cols = object_field.shape[1:]
    slots, pat = measured.shape[:2]
    modes = probe.shape[1]
    share = tile // nm
    chunks = min(4, share // 8)
    plain, turned = dft_tables(pat)
    f32, bf16 = jnp.float32, jnp.bfloat16
    vmem = pl.BlockSpec(memory_space=pltpu.VMEM)
    smem = pl.BlockSpec(memory_space=pltpu.SMEM)
    dma = pltpu.SemaphoreType.DMA
    others = nm - 1
    scratch = [
        pltpu.VMEM((2, 3 * tile, cols), f32),
        pltpu.VMEM((2, 3 * tile, cols), f32),
        pltpu.VMEM((3 * tile, cols), f32),
        pltpu.VMEM((slots, modes, 2 * pat, pat), bf16),
        pltpu.VMEM((slots, modes, pat, 2 * pat), f32),
        pltpu.VMEM((slots, pat, pat), f32),
        pltpu.VMEM((slots, others, pat, pat), f32),
        pltpu.VMEM((pat, pat), f32),
        pltpu.VMEM((others, pat, pat), f32),
        pltpu.VMEM((others, 3, 2, share, cols), f32),
        pltpu.VMEM((2, share, cols), f32),
        pltpu.VMEM((2, share, cols), f32),
        pltpu.VMEM((2, share, cols), f32),
        pltpu.VMEM((2, share, cols), f32),
        pltpu.VMEM((share, cols), f32),
        pltpu.VMEM((share, cols), f32),
        pltpu.VMEM((share, cols), f32),
        dma((chunks,)), dma((chunks,)), dma((chunks,)), dma((chunks,)),
        dma((others, chunks)), dma((others, chunks)), dma((others, chunks)), dma((others, chunks)),
        dma((slots, others)), dma((slots, others)), dma((others,)), dma((others,)),
        dma((1,)), dma((1,)), dma((1,)), dma((1,)),
        dma((others, 3)), dma((others, 3)),
        dma((chunks,)), dma((chunks,)), dma((chunks,)), dma((chunks,)),
    ]
    return pl.pallas_call(
        functools.partial(kernel, n, nm, chunks),
        out_shape=jax.ShapeDtypeStruct((2, share, cols), f32),
        in_specs=[smem] * 3 + [vmem] * 5,
        out_specs=vmem,
        scratch_shapes=scratch,
        compiler_params=pltpu.CompilerParams(
            collective_id=0, has_side_effects=True, vmem_limit_bytes=48 * 1024 * 1024
        ),
    )(
        row_offsets, col_offsets, tile_counts, object_field, probe, measured,
        jnp.asarray(plain), jnp.asarray(turned),
    )


def solution(mesh):
    in_specs = (
        P(None, "pos", None),
        P(None, "mode", None, None),
        P("pos", None, None),
        P("pos"),
        P("pos"),
        P("pos"),
    )
    out_specs = P(None, ("pos", "mode"), None)
    return jax.shard_map(local, mesh=mesh, in_specs=in_specs, out_specs=out_specs, check_vma=False)
```

```python
import functools
import math

import jax
import jax.numpy as jnp
import numpy as np
from jax import lax
from jax.experimental import pallas as pl
from jax.experimental.pallas import tpu as pltpu
from jax.sharding import PartitionSpec as P

MESH = pl.DeviceIdType.MESH


def dft_tables(pattern):
    counter = np.arange(pattern)
    angles = (counter[:, None] * counter[None, :] % pattern) * (2.0 * math.pi / pattern)
    factor = 1.0 / math.sqrt(pattern)
    real = (np.cos(angles) * factor).astype(np.float32)
    imag = (-np.sin(angles) * factor).astype(np.float32)
    plain = np.block([[real, -imag], [imag, real]]).astype(jnp.bfloat16)
    turned = np.block([[real, imag], [-imag, real]]).astype(jnp.bfloat16)
    return plain, turned


def kernel(
    n, nm, chunks,
    row_hbm, col_hbm, count_hbm, obj_hbm, probe_hbm, meas_hbm, plain_hbm, turned_hbm,
    out_ref,
    row_ref, col_ref, count_ref, probe_ref, meas_ref, plain_ref, turned_ref, load_s,
    ext, acc, illum, exit_ref, wave_ref, power, power_in, pp, pp_in, red_in,
    far_out, far_in, near_out, near_in, il_far_in, il_near_out, il_near_in,
    halo_s, halo_r, fwd_s, fwd_r, brn_s, brn_r, brf_s, brf_r,
    pow_s, pow_r, pp_s, pp_r, ilf_s, ilf_r, iln_s, iln_r,
    red_s, red_r, rf_s, rf_r, rn_s, rn_r,
):
    tile, cols = obj_hbm.shape[1], obj_hbm.shape[2]
    slots, pat = meas_ref.shape[0], meas_ref.shape[1]
    modes = probe_ref.shape[1]
    share = tile // nm
    piece = share // chunks
    lift = tile - pat // 2

    p = lax.axis_index("pos")
    m = lax.axis_index("mode")
    odd = lax.rem(p, 2)
    near_dev = p + 1 - 2 * odd
    far_blk = 2 * odd
    near_blk = 2 - far_blk
    far_raw = p - 2 + 4 * odd
    back_raw = p + 2 - 4 * odd
    has_far = jnp.logical_and(far_raw >= 0, far_raw < n)
    has_back = jnp.logical_and(back_raw >= 0, back_raw < n)
    far_dev = lax.rem(far_raw + n, n)
    back_dev = lax.rem(back_raw + n, n)
    others = [lax.rem(m + j, nm) for j in range(1, nm)]

    def rows_of(block, mode, c=0, size=None):
        size = share if size is None else size
        return pl.ds(pl.multiple_of(block * tile + mode * share + c * piece, 8), size)

    def remote(src, dst, s, r, pos, mode):
        return pltpu.make_async_remote_copy(
            src_ref=src, dst_ref=dst, send_sem=s, recv_sem=r,
            device_id=(pos, mode), device_id_type=MESH,
        )

    own = ext.at[:, tile : 2 * tile, :]
    pairs = (
        (probe_hbm, probe_ref), (row_hbm, row_ref), (col_hbm, col_ref), (count_hbm, count_ref),
        (obj_hbm, own), (plain_hbm, plain_ref), (turned_hbm, turned_ref), (meas_hbm, meas_ref),
    )
    loads = [pltpu.make_async_copy(a, b, load_s.at[i]) for i, (a, b) in enumerate(pairs)]
    barrier = pltpu.get_barrier_semaphore()
    pl.semaphore_signal(barrier, inc=1, device_id=(near_dev, m), device_id_type=MESH)
    for other in others:
        pl.semaphore_signal(barrier, inc=1, device_id=(p, other), device_id_type=MESH)

    @pl.when(has_far)
    def _():
        pl.semaphore_signal(barrier, inc=1, device_id=(far_dev, m), device_id_type=MESH)

    @pl.when(has_back)
    def _():
        pl.semaphore_signal(barrier, inc=1, device_id=(back_dev, m), device_id_type=MESH)

    greeted = has_far.astype(jnp.int32) + has_back.astype(jnp.int32)
    for load in loads:
        load.start()
    pl.semaphore_wait(barrier, nm + greeted)

    def halo(c):
        return remote(
            obj_hbm.at[:, rows_of(0, m, c, piece), :], ext.at[:, rows_of(far_blk, m, c, piece), :],
            halo_s.at[c], halo_r.at[c], near_dev, m,
        )

    def forward_near(c):
        return remote(
            ext.at[:, rows_of(near_blk, m, c, piece), :],
            ext.at[:, rows_of(far_blk, m, c, piece), :],
            fwd_s.at[c], fwd_r.at[c], back_dev, m,
        )

    def spread(block, c, j, s, r):
        where = rows_of(block, m, c, piece)
        return remote(
            ext.at[:, where, :], ext.at[:, where, :], s.at[j, c], r.at[j, c], p, others[j]
        )

    for c in range(chunks):
        halo(c).start()

    loads[0].wait()
    total = jnp.zeros((pat, pat), jnp.float32)
    for k in range(modes):
        total = total + probe_ref[0, k] * probe_ref[0, k] + probe_ref[1, k] * probe_ref[1, k]
    pp[...] = total

    def pp_copy(j):
        return remote(pp, pp_in.at[j], pp_s.at[j], pp_r.at[j], p, others[j])

    for j in range(nm - 1):
        pp_copy(j).start()

    for load in loads[1:]:
        load.wait()
    acc[...] = jnp.zeros_like(acc)
    illum[...] = jnp.zeros_like(illum)

    @pl.when(jnp.logical_not(has_far))
    def _():
        ext[:, pl.ds(pl.multiple_of(far_blk * tile, 8), tile), :] = jnp.zeros(
            (2, tile, cols), jnp.float32
        )

    for c in range(chunks):
        halo(c).wait_recv()

        @pl.when(has_back)
        def _():
            forward_near(c).start()

        for j in range(nm - 1):
            spread(near_blk, c, j, brn_s, brn_r).start()

    for j in range(nm - 1):
        pp_copy(j).wait_recv()

    live = count_ref[0]

    steps = []
    while sum(steps) < (3 * tile - pat) // 8 - 1:
        steps.insert(0, max(1, 2 * sum(steps[:1])))

    def placed(values, slot):
        top = lift + row_ref[slot]
        by = lax.rem(top, 8)
        groups = lax.div(top, 8)
        turned_rows = pltpu.roll(values.reshape(pat // 8, 8, pat), by, 1)
        blank = jnp.zeros((1, 8, pat), jnp.float32)
        upper = jnp.concatenate([turned_rows, blank], axis=0)
        lower = jnp.concatenate([blank, turned_rows], axis=0)
        line = lax.broadcasted_iota(jnp.int32, (1, 8, pat), 1)
        values = jnp.where(line >= by, upper, lower).reshape(pat + 8, pat)
        wide = jnp.concatenate([values, jnp.zeros((pat + 8, cols - pat), jnp.float32)], axis=1)
        wide = pltpu.roll(wide, col_ref[slot], 1).reshape(pat // 8 + 1, 8, cols)
        for step in reversed(steps):
            blank = jnp.zeros((step, 8, cols), jnp.float32)
            far = lax.rem(lax.div(groups, step), 2) == 1
            wide = jnp.where(
                far,
                jnp.concatenate([blank, wide], axis=0),
                jnp.concatenate([wide, blank], axis=0),
            )
        return wide.reshape(3 * tile, cols)

    def window(part, slot):
        top = lift + row_ref[slot]
        by = lax.rem(top, 8)
        groups = lax.div(top, 8)
        rows = ext[part].reshape(3 * tile // 8, 8, cols)
        for step in steps:
            far = lax.rem(lax.div(groups, step), 2) == 1
            rows = jnp.where(far, rows[step:], rows[:-step])
        turn = lax.rem(cols - col_ref[slot], cols)
        rows = pltpu.roll(rows.reshape(pat + 8, cols), turn, 1)
        rows = rows[:, :pat].reshape(pat // 8 + 1, 8, pat)
        rows = pltpu.roll(rows, lax.rem(8 - by, 8), 1)
        line = lax.broadcasted_iota(jnp.int32, (1, 8, pat), 1)
        return jnp.where(line < 8 - by, rows[:-1], rows[1:]).reshape(pat, pat)

    def add_illum(s, carry):
        whole = pp[...]
        for j in range(nm - 1):
            whole = whole + pp_in[j]
        whole = jnp.where(s < live, whole, 0.0)
        illum[...] += placed(whole, s)
        return carry

    lax.fori_loop(0, slots, add_illum, 0)

    @pl.when(has_far)
    def _():
        for c in range(chunks):
            forward_near(c).wait_recv()
            for j in range(nm - 1):
                spread(far_blk, c, j, brf_s, brf_r).start()

    def illum_far():
        return remote(
            illum.at[rows_of(far_blk, m), :], il_far_in, ilf_s.at[0], ilf_r.at[0], far_dev, m
        )

    def illum_near():
        return remote(il_near_out, il_near_in, iln_s.at[0], iln_r.at[0], near_dev, m)

    @pl.when(has_far)
    def _():
        illum_far().start()

    for c in range(chunks):
        for j in range(nm - 1):
            spread(near_blk, c, j, brn_s, brn_r).wait_recv()

    @pl.when(has_far)
    def _():
        for c in range(chunks):
            for j in range(nm - 1):
                spread(far_blk, c, j, brf_s, brf_r).wait_recv()

    def power_copy(s, j):
        return remote(
            power.at[s], power_in.at[s, j], pow_s.at[s, j], pow_r.at[s, j], p, others[j]
        )

    def forward(s, carry):
        win_re = window(0, s)
        win_im = window(1, s)
        model = jnp.zeros((pat, pat), jnp.float32)
        for k in range(modes):
            probe_re, probe_im = probe_ref[0, k], probe_ref[1, k]
            exit_re = (probe_re * win_re - probe_im * win_im).astype(jnp.bfloat16)
            exit_im = (probe_re * win_im + probe_im * win_re).astype(jnp.bfloat16)
            stacked = jnp.concatenate([exit_re, exit_im], axis=0)
            exit_ref[s, k] = stacked
            half = jnp.dot(plain_ref[...], stacked, preferred_element_type=jnp.float32)
            half = half.astype(jnp.bfloat16)
            half = jnp.concatenate([half[:pat], half[pat:]], axis=1)
            wave = jnp.dot(half, turned_ref[...], preferred_element_type=jnp.float32)
            wave_ref[s, k] = wave
            model = model + wave[:, :pat] * wave[:, :pat] + wave[:, pat:] * wave[:, pat:]
        power[s] = model
        for j in range(nm - 1):
            power_copy(s, j).start()
        return carry

    lax.fori_loop(0, slots, forward, 0)

    @pl.when(has_back)
    def _():
        illum_far().wait_recv()
        il_near_out[...] = illum[rows_of(near_blk, m), :] + il_far_in[...]

    @pl.when(jnp.logical_not(has_back))
    def _():
        il_near_out[...] = illum[rows_of(near_blk, m), :]

    illum_near().start()

    def backward(s, carry):
        model = power[s]
        for j in range(nm - 1):
            power_copy(s, j).wait_recv()
            model = model + power_in[s, j]
        scaling = jnp.sqrt(meas_ref[s]) / jnp.maximum(jnp.sqrt(model), 1.0)
        numer_re = jnp.zeros((pat, pat), jnp.float32)
        numer_im = jnp.zeros((pat, pat), jnp.float32)
        for k in range(modes):
            fixed_re = (scaling * wave_ref[s, k, :, :pat]).astype(jnp.bfloat16)
            fixed_im = (scaling * wave_ref[s, k, :, pat:]).astype(jnp.bfloat16)
            fixed = jnp.concatenate([fixed_re, fixed_im], axis=0)
            back = jnp.dot(turned_ref[...], fixed, preferred_element_type=jnp.float32)
            back = back.astype(jnp.bfloat16)
            back = jnp.concatenate([back[:pat], back[pat:]], axis=1)
            delta = jnp.dot(back, plain_ref[...], preferred_element_type=jnp.float32)
            delta_re = delta[:, :pat] - exit_ref[s, k, :pat, :].astype(jnp.float32)
            delta_im = delta[:, pat:] - exit_ref[s, k, pat:, :].astype(jnp.float32)
            probe_re, probe_im = probe_ref[0, k], probe_ref[1, k]
            numer_re = numer_re + probe_re * delta_re + probe_im * delta_im
            numer_im = numer_im + probe_re * delta_im - probe_im * delta_re
        on = s < live
        acc[0] += placed(jnp.where(on, numer_re, 0.0), s)
        acc[1] += placed(jnp.where(on, numer_im, 0.0), s)
        return carry

    lax.fori_loop(0, slots, backward, 0)

    blocks = (far_blk, near_blk, 1)

    def reduce_copy(b, j):
        return remote(
            acc.at[:, rows_of(blocks[b], others[j]), :], red_in.at[j, b],
            red_s.at[j, b], red_r.at[j, b], p, others[j],
        )

    for b in range(3):
        for j in range(nm - 1):
            reduce_copy(b, j).start()

    def reduced(b):
        value = acc[:, rows_of(blocks[b], m), :]
        for j in range(nm - 1):
            reduce_copy(b, j).wait_recv()
            value = value + red_in[j, b]
        return value

    def far_copy(c):
        part = pl.ds(c * piece, piece)
        return remote(
            far_out.at[:, part, :], far_in.at[:, part, :], rf_s.at[c], rf_r.at[c], far_dev, m
        )

    def near_copy(c):
        part = pl.ds(c * piece, piece)
        return remote(
            near_out.at[:, part, :], near_in.at[:, part, :], rn_s.at[c], rn_r.at[c], near_dev, m
        )

    far_out[...] = reduced(0)

    @pl.when(has_far)
    def _():
        for c in range(chunks):
            far_copy(c).start()

    near_out[...] = reduced(1)
    for c in range(chunks):

        @pl.when(has_back)
        def _():
            part = pl.ds(c * piece, piece)
            far_copy(c).wait_recv()
            near_out[:, part, :] = near_out[:, part, :] + far_in[:, part, :]

        near_copy(c).start()

    own_sum = reduced(2)
    illum_near().wait_recv()
    weight = 1.0 / (illum[rows_of(1, m), :] + il_near_in[...] + 1.0)
    for c in range(chunks):
        near_copy(c).wait_recv()
        part = slice(c * piece, (c + 1) * piece)
        out_ref[:, part, :] = ext[:, rows_of(1, m, c, piece), :] + (
            own_sum[:, part] + near_in[:, part, :]
        ) * weight[part]

    for c in range(chunks):
        halo(c).wait_send()
        near_copy(c).wait_send()
        for j in range(nm - 1):
            spread(near_blk, c, j, brn_s, brn_r).wait_send()
    for j in range(nm - 1):
        pp_copy(j).wait_send()
        for s in range(slots):
            power_copy(s, j).wait_send()
        for b in range(3):
            reduce_copy(b, j).wait_send()
    illum_near().wait_send()

    @pl.when(has_far)
    def _():
        illum_far().wait_send()
        for c in range(chunks):
            far_copy(c).wait_send()
            for j in range(nm - 1):
                spread(far_blk, c, j, brf_s, brf_r).wait_send()

    @pl.when(has_back)
    def _():
        for c in range(chunks):
            forward_near(c).wait_send()


def local(object_field, probe, measured, row_offsets, col_offsets, tile_counts):
    n, nm = lax.axis_size("pos"), lax.axis_size("mode")
    tile, cols = object_field.shape[1:]
    slots, pat = measured.shape[:2]
    modes = probe.shape[1]
    share = tile // nm
    chunks = min(4, share // 8)
    plain, turned = dft_tables(pat)
    f32, bf16 = jnp.float32, jnp.bfloat16
    vmem = pl.BlockSpec(memory_space=pltpu.VMEM)
    anywhere = pl.BlockSpec(memory_space=pl.ANY)
    dma = pltpu.SemaphoreType.DMA
    others = nm - 1
    scratch = [
        pltpu.SMEM((slots,), jnp.int32),
        pltpu.SMEM((slots,), jnp.int32),
        pltpu.SMEM((1,), jnp.int32),
        pltpu.VMEM((2, modes, pat, pat), f32),
        pltpu.VMEM((slots, pat, pat), f32),
        pltpu.VMEM((2 * pat, 2 * pat), bf16),
        pltpu.VMEM((2 * pat, 2 * pat), bf16),
        dma((8,)),
        pltpu.VMEM((2, 3 * tile, cols), f32),
        pltpu.VMEM((2, 3 * tile, cols), f32),
        pltpu.VMEM((3 * tile, cols), f32),
        pltpu.VMEM((slots, modes, 2 * pat, pat), bf16),
        pltpu.VMEM((slots, modes, pat, 2 * pat), f32),
        pltpu.VMEM((slots, pat, pat), f32),
        pltpu.VMEM((slots, others, pat, pat), f32),
        pltpu.VMEM((pat, pat), f32),
        pltpu.VMEM((others, pat, pat), f32),
        pltpu.VMEM((others, 3, 2, share, cols), f32),
        pltpu.VMEM((2, share, cols), f32),
        pltpu.VMEM((2, share, cols), f32),
        pltpu.VMEM((2, share, cols), f32),
        pltpu.VMEM((2, share, cols), f32),
        pltpu.VMEM((share, cols), f32),
        pltpu.VMEM((share, cols), f32),
        pltpu.VMEM((share, cols), f32),
        dma((chunks,)), dma((chunks,)), dma((chunks,)), dma((chunks,)),
        dma((others, chunks)), dma((others, chunks)), dma((others, chunks)), dma((others, chunks)),
        dma((slots, others)), dma((slots, others)), dma((others,)), dma((others,)),
        dma((1,)), dma((1,)), dma((1,)), dma((1,)),
        dma((others, 3)), dma((others, 3)),
        dma((chunks,)), dma((chunks,)), dma((chunks,)), dma((chunks,)),
    ]
    return pl.pallas_call(
        functools.partial(kernel, n, nm, chunks),
        out_shape=jax.ShapeDtypeStruct((2, share, cols), f32),
        in_specs=[anywhere] * 8,
        out_specs=vmem,
        scratch_shapes=scratch,
        compiler_params=pltpu.CompilerParams(
            collective_id=0, has_side_effects=True, vmem_limit_bytes=48 * 1024 * 1024
        ),
    )(
        row_offsets, col_offsets, tile_counts, object_field, probe, measured,
        jnp.asarray(plain), jnp.asarray(turned),
    )


def solution(mesh):
    in_specs = (
        P(None, "pos", None),
        P(None, "mode", None, None),
        P("pos", None, None),
        P("pos"),
        P("pos"),
        P("pos"),
    )
    out_specs = P(None, ("pos", "mode"), None)
    return jax.shard_map(local, mesh=mesh, in_specs=in_specs, out_specs=out_specs, check_vma=False)
```

```python
import functools
import math

import jax
import jax.numpy as jnp
from jax import lax
from jax.experimental import pallas as pl
from jax.experimental.pallas import tpu as pltpu
from jax.sharding import PartitionSpec as P

MESH = pl.DeviceIdType.MESH


def sine_of(step, period):
    step = jnp.bitwise_and(step, period - 1)
    step = jnp.where(step >= period // 2, step - period, step)
    step = jnp.where(step > period // 4, period // 2 - step, step)
    step = jnp.where(step < -(period // 4), -(period // 2) - step, step)
    x = step.astype(jnp.float32) * (2.0 * math.pi / period)
    y = x * x
    total = jnp.full_like(x, -1.0 / math.factorial(11))
    for order in (9, 7, 5, 3, 1):
        total = total * y + (-1.0) ** (order // 2) / math.factorial(order)
    return x * total


def dft_tables(pattern):
    rows = lax.broadcasted_iota(jnp.int32, (pattern, pattern), 0)
    columns = lax.broadcasted_iota(jnp.int32, (pattern, pattern), 1)
    phases = rows * columns
    factor = 1.0 / math.sqrt(pattern)
    real = sine_of(phases + pattern // 4, pattern) * factor
    imag = -sine_of(phases, pattern) * factor
    return real.astype(jnp.bfloat16), imag.astype(jnp.bfloat16), (-imag).astype(jnp.bfloat16)


def kernel(
    n, nm, chunks,
    row_hbm, col_hbm, count_hbm, obj_hbm, probe_hbm, meas_hbm,
    out_ref,
    row_ref, col_ref, count_ref, probe_ref, meas_ref, plain_ref, turned_ref, load_s,
    ext, acc, illum, exit_ref, wave_ref, power, power_in, pp, pp_in, red_in,
    far_out, far_in, near_out, near_in, il_far_in, il_near_out, il_near_in,
    halo_s, halo_r, fwd_s, fwd_r, brn_s, brn_r, brf_s, brf_r,
    pow_s, pow_r, pp_s, pp_r, ilf_s, ilf_r, iln_s, iln_r,
    red_s, red_r, rf_s, rf_r, rn_s, rn_r,
):
    tile, cols = obj_hbm.shape[1], obj_hbm.shape[2]
    slots, pat = meas_ref.shape[0], meas_ref.shape[1]
    modes = probe_ref.shape[1]
    share = tile // nm
    piece = share // chunks
    lift = tile - pat // 2

    p = lax.axis_index("pos")
    m = lax.axis_index("mode")
    odd = lax.rem(p, 2)
    near_dev = p + 1 - 2 * odd
    far_blk = 2 * odd
    near_blk = 2 - far_blk
    far_raw = p - 2 + 4 * odd
    back_raw = p + 2 - 4 * odd
    has_far = jnp.logical_and(far_raw >= 0, far_raw < n)
    has_back = jnp.logical_and(back_raw >= 0, back_raw < n)
    far_dev = lax.rem(far_raw + n, n)
    back_dev = lax.rem(back_raw + n, n)
    others = [lax.rem(m + j, nm) for j in range(1, nm)]

    def rows_of(block, mode, c=0, size=None):
        size = share if size is None else size
        return pl.ds(pl.multiple_of(block * tile + mode * share + c * piece, 8), size)

    def remote(src, dst, s, r, pos, mode):
        return pltpu.make_async_remote_copy(
            src_ref=src, dst_ref=dst, send_sem=s, recv_sem=r,
            device_id=(pos, mode), device_id_type=MESH,
        )

    own = ext.at[:, tile : 2 * tile, :]
    pairs = (
        (probe_hbm, probe_ref), (row_hbm, row_ref), (col_hbm, col_ref), (count_hbm, count_ref),
        (obj_hbm, own), (meas_hbm, meas_ref),
    )
    loads = [pltpu.make_async_copy(a, b, load_s.at[i]) for i, (a, b) in enumerate(pairs)]
    barrier = pltpu.get_barrier_semaphore()
    pl.semaphore_signal(barrier, inc=1, device_id=(near_dev, m), device_id_type=MESH)
    for other in others:
        pl.semaphore_signal(barrier, inc=1, device_id=(p, other), device_id_type=MESH)

    @pl.when(has_far)
    def _():
        pl.semaphore_signal(barrier, inc=1, device_id=(far_dev, m), device_id_type=MESH)

    @pl.when(has_back)
    def _():
        pl.semaphore_signal(barrier, inc=1, device_id=(back_dev, m), device_id_type=MESH)

    greeted = has_far.astype(jnp.int32) + has_back.astype(jnp.int32)
    for load in loads:
        load.start()
    pl.semaphore_wait(barrier, nm + greeted)

    def halo(c):
        return remote(
            obj_hbm.at[:, rows_of(0, m, c, piece), :], ext.at[:, rows_of(far_blk, m, c, piece), :],
            halo_s.at[c], halo_r.at[c], near_dev, m,
        )

    def forward_near(c):
        return remote(
            ext.at[:, rows_of(near_blk, m, c, piece), :],
            ext.at[:, rows_of(far_blk, m, c, piece), :],
            fwd_s.at[c], fwd_r.at[c], back_dev, m,
        )

    def spread(block, c, j, s, r):
        where = rows_of(block, m, c, piece)
        return remote(
            ext.at[:, where, :], ext.at[:, where, :], s.at[j, c], r.at[j, c], p, others[j]
        )

    for c in range(chunks):
        halo(c).start()

    loads[0].wait()
    total = jnp.zeros((pat, pat), jnp.float32)
    for k in range(modes):
        total = total + probe_ref[0, k] * probe_ref[0, k] + probe_ref[1, k] * probe_ref[1, k]
    pp[...] = total

    def pp_copy(j):
        return remote(pp, pp_in.at[j], pp_s.at[j], pp_r.at[j], p, others[j])

    for j in range(nm - 1):
        pp_copy(j).start()

    real, imag, flip = dft_tables(pat)
    for table, (high, low) in ((plain_ref, (flip, imag)), (turned_ref, (imag, flip))):
        table[:pat, :pat] = real
        table[pat:, pat:] = real
        table[:pat, pat:] = high
        table[pat:, :pat] = low
    for load in loads[1:]:
        load.wait()
    acc[...] = jnp.zeros_like(acc)
    illum[...] = jnp.zeros_like(illum)

    @pl.when(jnp.logical_not(has_far))
    def _():
        ext[:, pl.ds(pl.multiple_of(far_blk * tile, 8), tile), :] = jnp.zeros(
            (2, tile, cols), jnp.float32
        )

    for c in range(chunks):
        halo(c).wait_recv()

        @pl.when(has_back)
        def _():
            forward_near(c).start()

        for j in range(nm - 1):
            spread(near_blk, c, j, brn_s, brn_r).start()

    for j in range(nm - 1):
        pp_copy(j).wait_recv()

    live = count_ref[0]

    steps = []
    while sum(steps) < (3 * tile - pat) // 8 - 1:
        steps.insert(0, max(1, 2 * sum(steps[:1])))

    def placed(values, slot):
        top = lift + row_ref[slot]
        by = lax.rem(top, 8)
        groups = lax.div(top, 8)
        turned_rows = pltpu.roll(values.reshape(pat // 8, 8, pat), by, 1)
        blank = jnp.zeros((1, 8, pat), jnp.float32)
        upper = jnp.concatenate([turned_rows, blank], axis=0)
        lower = jnp.concatenate([blank, turned_rows], axis=0)
        line = lax.broadcasted_iota(jnp.int32, (1, 8, pat), 1)
        values = jnp.where(line >= by, upper, lower).reshape(pat + 8, pat)
        wide = jnp.concatenate([values, jnp.zeros((pat + 8, cols - pat), jnp.float32)], axis=1)
        wide = pltpu.roll(wide, col_ref[slot], 1).reshape(pat // 8 + 1, 8, cols)
        for step in reversed(steps):
            blank = jnp.zeros((step, 8, cols), jnp.float32)
            far = lax.rem(lax.div(groups, step), 2) == 1
            wide = jnp.where(
                far,
                jnp.concatenate([blank, wide], axis=0),
                jnp.concatenate([wide, blank], axis=0),
            )
        return wide.reshape(3 * tile, cols)

    def window(part, slot):
        top = lift + row_ref[slot]
        by = lax.rem(top, 8)
        groups = lax.div(top, 8)
        rows = ext[part].reshape(3 * tile // 8, 8, cols)
        for step in steps:
            far = lax.rem(lax.div(groups, step), 2) == 1
            rows = jnp.where(far, rows[step:], rows[:-step])
        turn = lax.rem(cols - col_ref[slot], cols)
        rows = pltpu.roll(rows.reshape(pat + 8, cols), turn, 1)
        rows = rows[:, :pat].reshape(pat // 8 + 1, 8, pat)
        rows = pltpu.roll(rows, lax.rem(8 - by, 8), 1)
        line = lax.broadcasted_iota(jnp.int32, (1, 8, pat), 1)
        return jnp.where(line < 8 - by, rows[:-1], rows[1:]).reshape(pat, pat)

    def add_illum(s, carry):
        whole = pp[...]
        for j in range(nm - 1):
            whole = whole + pp_in[j]
        whole = jnp.where(s < live, whole, 0.0)
        illum[...] += placed(whole, s)
        return carry

    lax.fori_loop(0, slots, add_illum, 0)

    @pl.when(has_far)
    def _():
        for c in range(chunks):
            forward_near(c).wait_recv()
            for j in range(nm - 1):
                spread(far_blk, c, j, brf_s, brf_r).start()

    def illum_far():
        return remote(
            illum.at[rows_of(far_blk, m), :], il_far_in, ilf_s.at[0], ilf_r.at[0], far_dev, m
        )

    def illum_near():
        return remote(il_near_out, il_near_in, iln_s.at[0], iln_r.at[0], near_dev, m)

    @pl.when(has_far)
    def _():
        illum_far().start()

    for c in range(chunks):
        for j in range(nm - 1):
            spread(near_blk, c, j, brn_s, brn_r).wait_recv()

    @pl.when(has_far)
    def _():
        for c in range(chunks):
            for j in range(nm - 1):
                spread(far_blk, c, j, brf_s, brf_r).wait_recv()

    def power_copy(s, j):
        return remote(
            power.at[s], power_in.at[s, j], pow_s.at[s, j], pow_r.at[s, j], p, others[j]
        )

    def forward(s, carry):
        win_re = window(0, s)
        win_im = window(1, s)
        model = jnp.zeros((pat, pat), jnp.float32)
        for k in range(modes):
            probe_re, probe_im = probe_ref[0, k], probe_ref[1, k]
            exit_re = (probe_re * win_re - probe_im * win_im).astype(jnp.bfloat16)
            exit_im = (probe_re * win_im + probe_im * win_re).astype(jnp.bfloat16)
            stacked = jnp.concatenate([exit_re, exit_im], axis=0)
            exit_ref[s, k] = stacked
            half = jnp.dot(plain_ref[...], stacked, preferred_element_type=jnp.float32)
            half = half.astype(jnp.bfloat16)
            half = jnp.concatenate([half[:pat], half[pat:]], axis=1)
            wave = jnp.dot(half, turned_ref[...], preferred_element_type=jnp.float32)
            wave_ref[s, k] = wave
            model = model + wave[:, :pat] * wave[:, :pat] + wave[:, pat:] * wave[:, pat:]
        power[s] = model
        for j in range(nm - 1):
            power_copy(s, j).start()
        return carry

    lax.fori_loop(0, slots, forward, 0)

    @pl.when(has_back)
    def _():
        illum_far().wait_recv()
        il_near_out[...] = illum[rows_of(near_blk, m), :] + il_far_in[...]

    @pl.when(jnp.logical_not(has_back))
    def _():
        il_near_out[...] = illum[rows_of(near_blk, m), :]

    illum_near().start()

    def backward(s, carry):
        model = power[s]
        for j in range(nm - 1):
            power_copy(s, j).wait_recv()
            model = model + power_in[s, j]
        scaling = jnp.sqrt(meas_ref[s]) / jnp.maximum(jnp.sqrt(model), 1.0)
        numer_re = jnp.zeros((pat, pat), jnp.float32)
        numer_im = jnp.zeros((pat, pat), jnp.float32)
        for k in range(modes):
            fixed_re = (scaling * wave_ref[s, k, :, :pat]).astype(jnp.bfloat16)
            fixed_im = (scaling * wave_ref[s, k, :, pat:]).astype(jnp.bfloat16)
            fixed = jnp.concatenate([fixed_re, fixed_im], axis=0)
            back = jnp.dot(turned_ref[...], fixed, preferred_element_type=jnp.float32)
            back = back.astype(jnp.bfloat16)
            back = jnp.concatenate([back[:pat], back[pat:]], axis=1)
            delta = jnp.dot(back, plain_ref[...], preferred_element_type=jnp.float32)
            delta_re = delta[:, :pat] - exit_ref[s, k, :pat, :].astype(jnp.float32)
            delta_im = delta[:, pat:] - exit_ref[s, k, pat:, :].astype(jnp.float32)
            probe_re, probe_im = probe_ref[0, k], probe_ref[1, k]
            numer_re = numer_re + probe_re * delta_re + probe_im * delta_im
            numer_im = numer_im + probe_re * delta_im - probe_im * delta_re
        on = s < live
        acc[0] += placed(jnp.where(on, numer_re, 0.0), s)
        acc[1] += placed(jnp.where(on, numer_im, 0.0), s)
        return carry

    lax.fori_loop(0, slots, backward, 0)

    blocks = (far_blk, near_blk, 1)

    def reduce_copy(b, j):
        return remote(
            acc.at[:, rows_of(blocks[b], others[j]), :], red_in.at[j, b],
            red_s.at[j, b], red_r.at[j, b], p, others[j],
        )

    for b in range(3):
        for j in range(nm - 1):
            reduce_copy(b, j).start()

    def reduced(b):
        value = acc[:, rows_of(blocks[b], m), :]
        for j in range(nm - 1):
            reduce_copy(b, j).wait_recv()
            value = value + red_in[j, b]
        return value

    def far_copy(c):
        part = pl.ds(c * piece, piece)
        return remote(
            far_out.at[:, part, :], far_in.at[:, part, :], rf_s.at[c], rf_r.at[c], far_dev, m
        )

    def near_copy(c):
        part = pl.ds(c * piece, piece)
        return remote(
            near_out.at[:, part, :], near_in.at[:, part, :], rn_s.at[c], rn_r.at[c], near_dev, m
        )

    far_out[...] = reduced(0)

    @pl.when(has_far)
    def _():
        for c in range(chunks):
            far_copy(c).start()

    near_out[...] = reduced(1)
    for c in range(chunks):

        @pl.when(has_back)
        def _():
            part = pl.ds(c * piece, piece)
            far_copy(c).wait_recv()
            near_out[:, part, :] = near_out[:, part, :] + far_in[:, part, :]

        near_copy(c).start()

    own_sum = reduced(2)
    illum_near().wait_recv()
    weight = 1.0 / (illum[rows_of(1, m), :] + il_near_in[...] + 1.0)
    for c in range(chunks):
        near_copy(c).wait_recv()
        part = slice(c * piece, (c + 1) * piece)
        out_ref[:, part, :] = ext[:, rows_of(1, m, c, piece), :] + (
            own_sum[:, part] + near_in[:, part, :]
        ) * weight[part]

    for c in range(chunks):
        halo(c).wait_send()
        near_copy(c).wait_send()
        for j in range(nm - 1):
            spread(near_blk, c, j, brn_s, brn_r).wait_send()
    for j in range(nm - 1):
        pp_copy(j).wait_send()
        for s in range(slots):
            power_copy(s, j).wait_send()
        for b in range(3):
            reduce_copy(b, j).wait_send()
    illum_near().wait_send()

    @pl.when(has_far)
    def _():
        illum_far().wait_send()
        for c in range(chunks):
            far_copy(c).wait_send()
            for j in range(nm - 1):
                spread(far_blk, c, j, brf_s, brf_r).wait_send()

    @pl.when(has_back)
    def _():
        for c in range(chunks):
            forward_near(c).wait_send()


def local(object_field, probe, measured, row_offsets, col_offsets, tile_counts):
    n, nm = lax.axis_size("pos"), lax.axis_size("mode")
    tile, cols = object_field.shape[1:]
    slots, pat = measured.shape[:2]
    modes = probe.shape[1]
    share = tile // nm
    chunks = min(4, share // 8)
    f32, bf16 = jnp.float32, jnp.bfloat16
    vmem = pl.BlockSpec(memory_space=pltpu.VMEM)
    anywhere = pl.BlockSpec(memory_space=pltpu.HBM)
    dma = pltpu.SemaphoreType.DMA
    others = nm - 1
    scratch = [
        pltpu.SMEM((slots,), jnp.int32),
        pltpu.SMEM((slots,), jnp.int32),
        pltpu.SMEM((1,), jnp.int32),
        pltpu.VMEM((2, modes, pat, pat), f32),
        pltpu.VMEM((slots, pat, pat), f32),
        pltpu.VMEM((2 * pat, 2 * pat), bf16),
        pltpu.VMEM((2 * pat, 2 * pat), bf16),
        dma((6,)),
        pltpu.VMEM((2, 3 * tile, cols), f32),
        pltpu.VMEM((2, 3 * tile, cols), f32),
        pltpu.VMEM((3 * tile, cols), f32),
        pltpu.VMEM((slots, modes, 2 * pat, pat), bf16),
        pltpu.VMEM((slots, modes, pat, 2 * pat), f32),
        pltpu.VMEM((slots, pat, pat), f32),
        pltpu.VMEM((slots, others, pat, pat), f32),
        pltpu.VMEM((pat, pat), f32),
        pltpu.VMEM((others, pat, pat), f32),
        pltpu.VMEM((others, 3, 2, share, cols), f32),
        pltpu.VMEM((2, share, cols), f32),
        pltpu.VMEM((2, share, cols), f32),
        pltpu.VMEM((2, share, cols), f32),
        pltpu.VMEM((2, share, cols), f32),
        pltpu.VMEM((share, cols), f32),
        pltpu.VMEM((share, cols), f32),
        pltpu.VMEM((share, cols), f32),
        dma((chunks,)), dma((chunks,)), dma((chunks,)), dma((chunks,)),
        dma((others, chunks)), dma((others, chunks)), dma((others, chunks)), dma((others, chunks)),
        dma((slots, others)), dma((slots, others)), dma((others,)), dma((others,)),
        dma((1,)), dma((1,)), dma((1,)), dma((1,)),
        dma((others, 3)), dma((others, 3)),
        dma((chunks,)), dma((chunks,)), dma((chunks,)), dma((chunks,)),
    ]
    return pl.pallas_call(
        functools.partial(kernel, n, nm, chunks),
        out_shape=jax.ShapeDtypeStruct((2, share, cols), f32),
        in_specs=[anywhere] * 6,
        out_specs=vmem,
        scratch_shapes=scratch,
        compiler_params=pltpu.CompilerParams(
            collective_id=0, has_side_effects=True, vmem_limit_bytes=64 * 1024 * 1024
        ),
    )(
        row_offsets, col_offsets, tile_counts, object_field, probe, measured
    )


def solution(mesh):
    in_specs = (
        P(None, "pos", None),
        P(None, "mode", None, None),
        P("pos", None, None),
        P("pos"),
        P("pos"),
        P("pos"),
    )
    out_specs = P(None, ("pos", "mode"), None)
    return jax.shard_map(local, mesh=mesh, in_specs=in_specs, out_specs=out_specs, check_vma=False)
```

```python
import functools
import math

import jax
import jax.numpy as jnp
from jax import lax
from jax.experimental import pallas as pl
from jax.experimental.pallas import tpu as pltpu
from jax.sharding import PartitionSpec as P

MESH = pl.DeviceIdType.MESH


def sine_of(step, period):
    step = jnp.bitwise_and(step, period - 1)
    step = jnp.where(step >= period // 2, step - period, step)
    step = jnp.where(step > period // 4, period // 2 - step, step)
    step = jnp.where(step < -(period // 4), -(period // 2) - step, step)
    x = step.astype(jnp.float32) * (2.0 * math.pi / period)
    y = x * x
    total = jnp.full_like(x, -1.0 / math.factorial(11))
    for order in (9, 7, 5, 3, 1):
        total = total * y + (-1.0) ** (order // 2) / math.factorial(order)
    return x * total


def dft_tables(pattern):
    rows = lax.broadcasted_iota(jnp.int32, (pattern, pattern), 0)
    columns = lax.broadcasted_iota(jnp.int32, (pattern, pattern), 1)
    phases = rows * columns
    factor = 1.0 / math.sqrt(pattern)
    real = sine_of(phases + pattern // 4, pattern) * factor
    imag = -sine_of(phases, pattern) * factor
    return real, imag


def kernel(
    n, nm, chunks,
    row_hbm, col_hbm, count_hbm, obj_hbm, probe_hbm, meas_hbm,
    out_ref,
    row_ref, col_ref, count_ref, probe_ref, meas_ref, plain_ref, turned_ref, load_s,
    base, left, right, spun, early, stage, ext, acc, illum, exit_ref, wave_ref, power, power_in, pp, pp_in, red_in,
    far_out, far_in, near_out, near_in, il_far_in, il_near_out, il_near_in,
    halo_s, halo_r, fwd_s, fwd_r, brn_s, brn_r, brf_s, brf_r,
    pow_s, pow_r, pp_s, pp_r, ilf_s, ilf_r, iln_s, iln_r,
    red_s, red_r, rf_s, rf_r, rn_s, rn_r,
):
    tile, cols = obj_hbm.shape[1], obj_hbm.shape[2]
    slots, pat = meas_ref.shape[0], meas_ref.shape[1]
    modes = probe_ref.shape[1]
    share = tile // nm
    piece = share // chunks
    assert pat == 2 * tile
    f32, bf16 = jnp.float32, jnp.bfloat16

    p = lax.axis_index("pos")
    m = lax.axis_index("mode")
    odd = lax.rem(p, 2)
    near_dev = p + 1 - 2 * odd
    far_blk = 2 * odd
    near_blk = 2 - far_blk
    far_raw = p - 2 + 4 * odd
    back_raw = p + 2 - 4 * odd
    has_far = jnp.logical_and(far_raw >= 0, far_raw < n)
    has_back = jnp.logical_and(back_raw >= 0, back_raw < n)
    far_dev = lax.rem(far_raw + n, n)
    back_dev = lax.rem(back_raw + n, n)
    others = [lax.rem(m + j, nm) for j in range(1, nm)]

    def rows_of(block, mode, c=0, size=None):
        size = share if size is None else size
        return pl.ds(pl.multiple_of(block * tile + mode * share + c * piece, 8), size)

    def remote(src, dst, s, r, pos, mode):
        return pltpu.make_async_remote_copy(
            src_ref=src, dst_ref=dst, send_sem=s, recv_sem=r,
            device_id=(pos, mode), device_id_type=MESH,
        )

    own = ext.at[:, tile : 2 * tile, :]
    pairs = (
        (probe_hbm, probe_ref), (row_hbm, row_ref), (col_hbm, col_ref), (count_hbm, count_ref),
        (obj_hbm, own), (meas_hbm, meas_ref),
    )
    loads = [pltpu.make_async_copy(a, b, load_s.at[i]) for i, (a, b) in enumerate(pairs)]
    def fill(table, real, imag, sign):
        high, wide = table.shape[0] // 2, table.shape[1] // 2
        real = real.astype(jnp.bfloat16)
        table[:high, :wide] = real
        table[high:, wide:] = real
        table[:high, wide:] = (sign * imag).astype(jnp.bfloat16)
        table[high:, :wide] = (-sign * imag).astype(jnp.bfloat16)

    barrier = pltpu.get_barrier_semaphore()
    pl.semaphore_signal(barrier, inc=1, device_id=(near_dev, m), device_id_type=MESH)
    for other in others:
        pl.semaphore_signal(barrier, inc=1, device_id=(p, other), device_id_type=MESH)

    @pl.when(has_far)
    def _():
        pl.semaphore_signal(barrier, inc=1, device_id=(far_dev, m), device_id_type=MESH)

    @pl.when(has_back)
    def _():
        pl.semaphore_signal(barrier, inc=1, device_id=(back_dev, m), device_id_type=MESH)

    greeted = has_far.astype(jnp.int32) + has_back.astype(jnp.int32)
    for load in loads:
        load.start()
    pl.semaphore_wait(barrier, nm + greeted)

    def halo(c):
        return remote(
            obj_hbm.at[:, rows_of(0, m, c, piece), :], ext.at[:, rows_of(far_blk, m, c, piece), :],
            halo_s.at[c], halo_r.at[c], near_dev, m,
        )

    def forward_near(c):
        return remote(
            ext.at[:, rows_of(near_blk, m, c, piece), :],
            ext.at[:, rows_of(far_blk, m, c, piece), :],
            fwd_s.at[c], fwd_r.at[c], back_dev, m,
        )

    def spread(block, c, j, s, r):
        where = rows_of(block, m, c, piece)
        return remote(
            ext.at[:, where, :], ext.at[:, where, :], s.at[j, c], r.at[j, c], p, others[j]
        )

    for c in range(chunks):
        halo(c).start()

    loads[0].wait()
    total = jnp.zeros((pat, pat), jnp.float32)
    for k in range(modes):
        total = total + probe_ref[0, k] * probe_ref[0, k] + probe_ref[1, k] * probe_ref[1, k]
    pp[...] = total

    def pp_copy(j):
        return remote(pp, pp_in.at[j], pp_s.at[j], pp_r.at[j], p, others[j])

    for j in range(nm - 1):
        pp_copy(j).start()

    real, imag = dft_tables(pat)
    base[0] = real
    base[1] = imag
    for table, sign in ((plain_ref, -1.0), (turned_ref, 1.0)):
        fill(table, real, imag, sign)
    for load in loads[1:]:
        load.wait()
    acc[...] = jnp.zeros_like(acc)
    illum[...] = jnp.zeros_like(illum)

    @pl.when(jnp.logical_not(has_far))
    def _():
        ext[:, pl.ds(pl.multiple_of(far_blk * tile, 8), tile), :] = jnp.zeros(
            (2, tile, cols), jnp.float32
        )

    line = lax.broadcasted_iota(jnp.int32, (tile, cols), 0)

    def narrowed(rows, slot):
        return pltpu.roll(rows, lax.rem(cols - col_ref[slot], cols), 1)[:, :pat]

    def add_placed(total, values, slot):
        wide = jnp.concatenate([values, jnp.zeros((pat, cols - pat), f32)], axis=1)
        wide = pltpu.roll(wide, col_ref[slot], 1)
        outer, below = wide[:tile], line < row_ref[slot]
        total[:tile, :] += jnp.where(below, 0.0, outer)
        total[tile : 2 * tile, :] += wide[tile:]
        total[2 * tile :, :] += jnp.where(below, outer, 0.0)

    def exits(s, k, part, win_re, win_im):
        rows = slice(part * tile, (part + 1) * tile)
        probe_re, probe_im = spun[s, 0, k, rows, :], spun[s, 1, k, rows, :]
        exit_re = (probe_re * win_re - probe_im * win_im).astype(bf16)
        exit_im = (probe_re * win_im + probe_im * win_re).astype(bf16)
        stacked = jnp.concatenate([exit_re, exit_im], axis=0)
        exit_ref[s, k, part] = stacked
        return jnp.dot(left[s, part], stacked, preferred_element_type=f32)

    def prepare(s):
        shift = row_ref[s]
        real, imag = (pltpu.roll(base[i], shift, 1) for i in (0, 1))
        for part in (0, 1):
            columns = slice(part * tile, (part + 1) * tile)
            fill(left.at[s, part], real[:, columns], imag[:, columns], -1.0)
        fill(right.at[s], pltpu.roll(base[0], shift, 0), pltpu.roll(base[1], shift, 0), 1.0)
        for i in (0, 1):
            for k in range(modes):
                spun[s, i, k] = pltpu.roll(probe_ref[i, k], shift, 0)
        win_re = narrowed(ext[0, tile : 2 * tile, :], s)
        win_im = narrowed(ext[1, tile : 2 * tile, :], s)
        for k in range(modes):
            early[s, k] = exits(s, k, 1, win_re, win_im)

    for c in range(max(chunks, slots)):
        if c < slots:
            prepare(c)
        if c >= chunks:
            continue
        halo(c).wait_recv()

        @pl.when(has_back)
        def _():
            forward_near(c).start()

        for j in range(nm - 1):
            spread(near_blk, c, j, brn_s, brn_r).start()

    for j in range(nm - 1):
        pp_copy(j).wait_recv()

    live = count_ref[0]

    def add_illum(s, carry):
        whole = pp[...]
        for j in range(nm - 1):
            whole = whole + pp_in[j]
        whole = jnp.where(s < live, whole, 0.0)
        add_placed(illum, pltpu.roll(whole, row_ref[s], 0), s)
        return carry

    def relay(c):
        @pl.when(has_far)
        def _():
            forward_near(c).wait_recv()
            for j in range(nm - 1):
                spread(far_blk, c, j, brf_s, brf_r).start()

    for c in range(chunks - 1):
        relay(c)
    lax.fori_loop(0, slots, add_illum, 0)
    relay(chunks - 1)

    def illum_far():
        return remote(
            illum.at[rows_of(far_blk, m), :], il_far_in, ilf_s.at[0], ilf_r.at[0], far_dev, m
        )

    def illum_near():
        return remote(il_near_out, il_near_in, iln_s.at[0], iln_r.at[0], near_dev, m)

    @pl.when(has_far)
    def _():
        illum_far().start()

    for c in range(chunks):
        for j in range(nm - 1):
            spread(near_blk, c, j, brn_s, brn_r).wait_recv()

    @pl.when(has_far)
    def _():
        for c in range(chunks):
            for j in range(nm - 1):
                spread(far_blk, c, j, brf_s, brf_r).wait_recv()

    def power_copy(s, j):
        return remote(
            power.at[s], power_in.at[s, j], pow_s.at[s, j], pow_r.at[s, j], p, others[j]
        )

    def forward(s, carry):
        below = line < row_ref[s]
        win_re, win_im = (
            narrowed(jnp.where(below, ext[i, 2 * tile :, :], ext[i, :tile, :]), s) for i in (0, 1)
        )
        for k in range(modes):
            half = early[s, k] + exits(s, k, 0, win_re, win_im)
            half = half.astype(bf16)
            stage[k * pat : (k + 1) * pat, :pat] = half[:pat]
            stage[k * pat : (k + 1) * pat, pat:] = half[pat:]
        wave_ref[s] = jnp.dot(stage[...], turned_ref[...], preferred_element_type=f32)
        model = jnp.zeros((pat, pat), f32)
        for k in range(modes):
            wave = wave_ref[s, k * pat : (k + 1) * pat, :]
            model = model + wave[:, :pat] * wave[:, :pat] + wave[:, pat:] * wave[:, pat:]
        power[s] = model
        for j in range(nm - 1):
            power_copy(s, j).start()
        return carry

    lax.fori_loop(0, slots, forward, 0)

    @pl.when(has_back)
    def _():
        illum_far().wait_recv()
        il_near_out[...] = illum[rows_of(near_blk, m), :] + il_far_in[...]

    @pl.when(jnp.logical_not(has_back))
    def _():
        il_near_out[...] = illum[rows_of(near_blk, m), :]

    illum_near().start()

    def backward(s, carry):
        model = power[s]
        for j in range(nm - 1):
            power_copy(s, j).wait_recv()
            model = model + power_in[s, j]
        scaling = jnp.sqrt(meas_ref[s]) / jnp.maximum(jnp.sqrt(model), 1.0)
        numer_re = jnp.zeros((pat, pat), jnp.float32)
        numer_im = jnp.zeros((pat, pat), jnp.float32)
        for k in range(modes):
            block = slice(k * pat, (k + 1) * pat)
            fixed_re = (scaling * wave_ref[s, block, :pat]).astype(bf16)
            fixed_im = (scaling * wave_ref[s, block, pat:]).astype(bf16)
            fixed = jnp.concatenate([fixed_re, fixed_im], axis=0)
            back = jnp.dot(right[s], fixed, preferred_element_type=f32).astype(bf16)
            stage[block, :pat] = back[:pat]
            stage[block, pat:] = back[pat:]
        wave_ref[s] = jnp.dot(stage[...], plain_ref[...], preferred_element_type=f32)
        for k in range(modes):
            delta = wave_ref[s, k * pat : (k + 1) * pat, :]
            exit_re = jnp.concatenate([exit_ref[s, k, i, :tile, :] for i in (0, 1)], axis=0)
            exit_im = jnp.concatenate([exit_ref[s, k, i, tile:, :] for i in (0, 1)], axis=0)
            delta_re = delta[:, :pat] - exit_re.astype(f32)
            delta_im = delta[:, pat:] - exit_im.astype(f32)
            probe_re, probe_im = spun[s, 0, k], spun[s, 1, k]
            numer_re = numer_re + probe_re * delta_re + probe_im * delta_im
            numer_im = numer_im + probe_re * delta_im - probe_im * delta_re
        on = s < live
        add_placed(acc.at[0], jnp.where(on, numer_re, 0.0), s)
        add_placed(acc.at[1], jnp.where(on, numer_im, 0.0), s)
        return carry

    lax.fori_loop(0, slots, backward, 0)

    blocks = (far_blk, near_blk, 1)

    def reduce_copy(b, j):
        return remote(
            acc.at[:, rows_of(blocks[b], others[j]), :], red_in.at[j, b],
            red_s.at[j, b], red_r.at[j, b], p, others[j],
        )

    for b in range(3):
        for j in range(nm - 1):
            reduce_copy(b, j).start()

    def reduced(b):
        value = acc[:, rows_of(blocks[b], m), :]
        for j in range(nm - 1):
            reduce_copy(b, j).wait_recv()
            value = value + red_in[j, b]
        return value

    def far_copy(c):
        part = pl.ds(c * piece, piece)
        return remote(
            far_out.at[:, part, :], far_in.at[:, part, :], rf_s.at[c], rf_r.at[c], far_dev, m
        )

    def near_copy(c):
        part = pl.ds(c * piece, piece)
        return remote(
            near_out.at[:, part, :], near_in.at[:, part, :], rn_s.at[c], rn_r.at[c], near_dev, m
        )

    far_out[...] = reduced(0)

    @pl.when(has_far)
    def _():
        for c in range(chunks):
            far_copy(c).start()

    near_out[...] = reduced(1)
    for c in range(chunks):

        @pl.when(has_back)
        def _():
            part = pl.ds(c * piece, piece)
            far_copy(c).wait_recv()
            near_out[:, part, :] = near_out[:, part, :] + far_in[:, part, :]

        near_copy(c).start()

    own_sum = reduced(2)
    illum_near().wait_recv()
    weight = 1.0 / (illum[rows_of(1, m), :] + il_near_in[...] + 1.0)
    for c in range(chunks):
        near_copy(c).wait_recv()
        part = slice(c * piece, (c + 1) * piece)
        out_ref[:, part, :] = ext[:, rows_of(1, m, c, piece), :] + (
            own_sum[:, part] + near_in[:, part, :]
        ) * weight[part]

    for c in range(chunks):
        halo(c).wait_send()
        near_copy(c).wait_send()
        for j in range(nm - 1):
            spread(near_blk, c, j, brn_s, brn_r).wait_send()
    for j in range(nm - 1):
        pp_copy(j).wait_send()
        for s in range(slots):
            power_copy(s, j).wait_send()
        for b in range(3):
            reduce_copy(b, j).wait_send()
    illum_near().wait_send()

    @pl.when(has_far)
    def _():
        illum_far().wait_send()
        for c in range(chunks):
            far_copy(c).wait_send()
            for j in range(nm - 1):
                spread(far_blk, c, j, brf_s, brf_r).wait_send()

    @pl.when(has_back)
    def _():
        for c in range(chunks):
            forward_near(c).wait_send()


def local(object_field, probe, measured, row_offsets, col_offsets, tile_counts):
    n, nm = lax.axis_size("pos"), lax.axis_size("mode")
    tile, cols = object_field.shape[1:]
    slots, pat = measured.shape[:2]
    modes = probe.shape[1]
    share = tile // nm
    chunks = min(4, share // 8)
    f32, bf16 = jnp.float32, jnp.bfloat16
    vmem = pl.BlockSpec(memory_space=pltpu.VMEM)
    anywhere = pl.BlockSpec(memory_space=pltpu.HBM)
    dma = pltpu.SemaphoreType.DMA
    others = nm - 1
    scratch = [
        pltpu.SMEM((slots,), jnp.int32),
        pltpu.SMEM((slots,), jnp.int32),
        pltpu.SMEM((1,), jnp.int32),
        pltpu.VMEM((2, modes, pat, pat), f32),
        pltpu.VMEM((slots, pat, pat), f32),
        pltpu.VMEM((2 * pat, 2 * pat), bf16),
        pltpu.VMEM((2 * pat, 2 * pat), bf16),
        dma((6,)),
        pltpu.VMEM((2, pat, pat), f32),
        pltpu.VMEM((slots, 2, 2 * pat, pat), bf16),
        pltpu.VMEM((slots, 2 * pat, 2 * pat), bf16),
        pltpu.VMEM((slots, 2, modes, pat, pat), f32),
        pltpu.VMEM((slots, modes, 2 * pat, pat), f32),
        pltpu.VMEM((modes * pat, 2 * pat), bf16),
        pltpu.VMEM((2, 3 * tile, cols), f32),
        pltpu.VMEM((2, 3 * tile, cols), f32),
        pltpu.VMEM((3 * tile, cols), f32),
        pltpu.VMEM((slots, modes, 2, pat, pat), bf16),
        pltpu.VMEM((slots, modes * pat, 2 * pat), f32),
        pltpu.VMEM((slots, pat, pat), f32),
        pltpu.VMEM((slots, others, pat, pat), f32),
        pltpu.VMEM((pat, pat), f32),
        pltpu.VMEM((others, pat, pat), f32),
        pltpu.VMEM((others, 3, 2, share, cols), f32),
        pltpu.VMEM((2, share, cols), f32),
        pltpu.VMEM((2, share, cols), f32),
        pltpu.VMEM((2, share, cols), f32),
        pltpu.VMEM((2, share, cols), f32),
        pltpu.VMEM((share, cols), f32),
        pltpu.VMEM((share, cols), f32),
        pltpu.VMEM((share, cols), f32),
        dma((chunks,)), dma((chunks,)), dma((chunks,)), dma((chunks,)),
        dma((others, chunks)), dma((others, chunks)), dma((others, chunks)), dma((others, chunks)),
        dma((slots, others)), dma((slots, others)), dma((others,)), dma((others,)),
        dma((1,)), dma((1,)), dma((1,)), dma((1,)),
        dma((others, 3)), dma((others, 3)),
        dma((chunks,)), dma((chunks,)), dma((chunks,)), dma((chunks,)),
    ]
    return pl.pallas_call(
        functools.partial(kernel, n, nm, chunks),
        out_shape=jax.ShapeDtypeStruct((2, share, cols), f32),
        in_specs=[anywhere] * 6,
        out_specs=vmem,
        scratch_shapes=scratch,
        compiler_params=pltpu.CompilerParams(
            collective_id=0, has_side_effects=True, vmem_limit_bytes=64 * 1024 * 1024
        ),
    )(
        row_offsets, col_offsets, tile_counts, object_field, probe, measured
    )


def solution(mesh):
    in_specs = (
        P(None, "pos", None),
        P(None, "mode", None, None),
        P("pos", None, None),
        P("pos"),
        P("pos"),
        P("pos"),
    )
    out_specs = P(None, ("pos", "mode"), None)
    return jax.shard_map(local, mesh=mesh, in_specs=in_specs, out_specs=out_specs, check_vma=False)
```

```python
import functools
import math

import jax
import jax.numpy as jnp
from jax import lax
from jax.experimental import pallas as pl
from jax.experimental.pallas import tpu as pltpu
from jax.sharding import PartitionSpec as P

MESH = pl.DeviceIdType.MESH


def sine_of(step, period):
    step = jnp.bitwise_and(step, period - 1)
    step = jnp.where(step >= period // 2, step - period, step)
    step = jnp.where(step > period // 4, period // 2 - step, step)
    step = jnp.where(step < -(period // 4), -(period // 2) - step, step)
    x = step.astype(jnp.float32) * (2.0 * math.pi / period)
    y = x * x
    total = jnp.full_like(x, -1.0 / math.factorial(11))
    for order in (9, 7, 5, 3, 1):
        total = total * y + (-1.0) ** (order // 2) / math.factorial(order)
    return x * total


def dft_tables(pattern):
    rows = lax.broadcasted_iota(jnp.int32, (pattern, pattern), 0)
    columns = lax.broadcasted_iota(jnp.int32, (pattern, pattern), 1)
    phases = rows * columns
    factor = 1.0 / math.sqrt(pattern)
    real = sine_of(phases + pattern // 4, pattern) * factor
    imag = -sine_of(phases, pattern) * factor
    return real, imag


def kernel(
    n, nm, chunks,
    row_hbm, col_hbm, count_hbm, obj_hbm, probe_hbm, meas_hbm,
    out_ref,
    row_ref, col_ref, count_ref, probe_ref, meas_ref, plain_ref, turned_ref, load_s,
    base, left, right, fixed_ref, spun, early, stage, delta_ref, ext, acc, illum, exit_ref, wave_ref, power, power_in, pp, pp_in, red_in,
    far_out, far_in, near_out, near_in, il_far_in, il_near_out, il_near_in,
    halo_s, halo_r, fwd_s, fwd_r, brn_s, brn_r, brf_s, brf_r,
    pow_s, pow_r, pp_s, pp_r, ilf_s, ilf_r, iln_s, iln_r,
    red_s, red_r, rf_s, rf_r, rn_s, rn_r,
):
    tile, cols = obj_hbm.shape[1], obj_hbm.shape[2]
    slots, pat = meas_ref.shape[0], meas_ref.shape[1]
    modes = probe_ref.shape[1]
    share = tile // nm
    piece = share // chunks
    assert pat == 2 * tile
    f32, bf16 = jnp.float32, jnp.bfloat16

    p = lax.axis_index("pos")
    m = lax.axis_index("mode")
    odd = lax.rem(p, 2)
    near_dev = p + 1 - 2 * odd
    far_blk = 2 * odd
    near_blk = 2 - far_blk
    far_raw = p - 2 + 4 * odd
    back_raw = p + 2 - 4 * odd
    has_far = jnp.logical_and(far_raw >= 0, far_raw < n)
    has_back = jnp.logical_and(back_raw >= 0, back_raw < n)
    far_dev = lax.rem(far_raw + n, n)
    back_dev = lax.rem(back_raw + n, n)
    others = [lax.rem(m + j, nm) for j in range(1, nm)]

    def rows_of(block, mode, c=0, size=None):
        size = share if size is None else size
        return pl.ds(pl.multiple_of(block * tile + mode * share + c * piece, 8), size)

    def remote(src, dst, s, r, pos, mode):
        return pltpu.make_async_remote_copy(
            src_ref=src, dst_ref=dst, send_sem=s, recv_sem=r,
            device_id=(pos, mode), device_id_type=MESH,
        )

    own = ext.at[:, tile : 2 * tile, :]
    pairs = (
        (probe_hbm, probe_ref), (row_hbm, row_ref), (col_hbm, col_ref), (count_hbm, count_ref),
        (obj_hbm, own), (meas_hbm, meas_ref),
    )
    loads = [pltpu.make_async_copy(a, b, load_s.at[i]) for i, (a, b) in enumerate(pairs)]
    def fill(table, real, imag, sign):
        high, wide = table.shape[0] // 2, table.shape[1] // 2
        real = real.astype(jnp.bfloat16)
        table[:high, :wide] = real
        table[high:, wide:] = real
        table[:high, wide:] = (sign * imag).astype(jnp.bfloat16)
        table[high:, :wide] = (-sign * imag).astype(jnp.bfloat16)

    barrier = pltpu.get_barrier_semaphore()
    pl.semaphore_signal(barrier, inc=1, device_id=(near_dev, m), device_id_type=MESH)
    for other in others:
        pl.semaphore_signal(barrier, inc=1, device_id=(p, other), device_id_type=MESH)

    @pl.when(has_far)
    def _():
        pl.semaphore_signal(barrier, inc=1, device_id=(far_dev, m), device_id_type=MESH)

    @pl.when(has_back)
    def _():
        pl.semaphore_signal(barrier, inc=1, device_id=(back_dev, m), device_id_type=MESH)

    greeted = has_far.astype(jnp.int32) + has_back.astype(jnp.int32)
    for load in loads:
        load.start()
    pl.semaphore_wait(barrier, nm + greeted)

    def halo(c):
        return remote(
            obj_hbm.at[:, rows_of(0, m, c, piece), :], ext.at[:, rows_of(far_blk, m, c, piece), :],
            halo_s.at[c], halo_r.at[c], near_dev, m,
        )

    def forward_near(c):
        return remote(
            ext.at[:, rows_of(near_blk, m, c, piece), :],
            ext.at[:, rows_of(far_blk, m, c, piece), :],
            fwd_s.at[c], fwd_r.at[c], back_dev, m,
        )

    def spread(block, c, j, s, r):
        where = rows_of(block, m, c, piece)
        return remote(
            ext.at[:, where, :], ext.at[:, where, :], s.at[j, c], r.at[j, c], p, others[j]
        )

    for c in range(chunks):
        halo(c).start()

    loads[0].wait()
    total = jnp.zeros((pat, pat), jnp.float32)
    for k in range(modes):
        total = total + probe_ref[0, k] * probe_ref[0, k] + probe_ref[1, k] * probe_ref[1, k]
    pp[...] = total

    def pp_copy(j):
        return remote(pp, pp_in.at[j], pp_s.at[j], pp_r.at[j], p, others[j])

    for j in range(nm - 1):
        pp_copy(j).start()

    real, imag = dft_tables(pat)
    base[0] = real
    base[1] = imag
    for table, sign in ((plain_ref, -1.0), (turned_ref, 1.0)):
        fill(table, real, imag, sign)
    for load in loads[1:]:
        load.wait()
    acc[...] = jnp.zeros_like(acc)
    illum[...] = jnp.zeros_like(illum)

    @pl.when(jnp.logical_not(has_far))
    def _():
        ext[:, pl.ds(pl.multiple_of(far_blk * tile, 8), tile), :] = jnp.zeros(
            (2, tile, cols), jnp.float32
        )

    line = lax.broadcasted_iota(jnp.int32, (tile, cols), 0)

    def narrowed(rows, slot):
        return pltpu.roll(rows, lax.rem(cols - col_ref[slot], cols), 1)[:, :pat]

    def widened(values, slot):
        blank = jnp.zeros((tile, cols - pat), f32)
        return pltpu.roll(jnp.concatenate([values, blank], axis=1), col_ref[slot], 1)

    def add_outer(total, values, slot):
        wide, below = widened(values, slot), line < row_ref[slot]
        total[:tile, :] += jnp.where(below, 0.0, wide)
        total[2 * tile :, :] += jnp.where(below, wide, 0.0)

    def add_inner(total, values, slot):
        total[tile : 2 * tile, :] += widened(values, slot)

    def exits(s, k, part, win_re, win_im):
        rows = slice(part * tile, (part + 1) * tile)
        probe_re, probe_im = spun[s, 0, k, rows, :], spun[s, 1, k, rows, :]
        exit_re = (probe_re * win_re - probe_im * win_im).astype(bf16)
        exit_im = (probe_re * win_im + probe_im * win_re).astype(bf16)
        stacked = jnp.concatenate([exit_re, exit_im], axis=0)
        exit_ref[s, k, part] = stacked
        return jnp.dot(left[s, part], stacked, preferred_element_type=f32)

    def prepare(s):
        shift = row_ref[s]
        real, imag = (pltpu.roll(base[i], shift, 1) for i in (0, 1))
        for part in (0, 1):
            columns = slice(part * tile, (part + 1) * tile)
            fill(left.at[s, part], real[:, columns], imag[:, columns], -1.0)
        real, imag = (pltpu.roll(base[i], shift, 0) for i in (0, 1))
        for part in (0, 1):
            rows = slice(part * tile, (part + 1) * tile)
            fill(right.at[s, part], real[rows], imag[rows], 1.0)
        for i in (0, 1):
            for k in range(modes):
                spun[s, i, k] = pltpu.roll(probe_ref[i, k], shift, 0)
        win_re = narrowed(ext[0, tile : 2 * tile, :], s)
        win_im = narrowed(ext[1, tile : 2 * tile, :], s)
        for k in range(modes):
            early[s, k] = exits(s, k, 1, win_re, win_im)

    for c in range(max(chunks, slots)):
        if c < slots:
            prepare(c)
        if c >= chunks:
            continue
        halo(c).wait_recv()

        @pl.when(has_back)
        def _():
            forward_near(c).start()

        for j in range(nm - 1):
            spread(near_blk, c, j, brn_s, brn_r).start()

    for j in range(nm - 1):
        pp_copy(j).wait_recv()

    live = count_ref[0]

    def add_illum(s, carry):
        whole = pp[...]
        for j in range(nm - 1):
            whole = whole + pp_in[j]
        whole = jnp.where(s < live, whole, 0.0)
        whole = pltpu.roll(whole, row_ref[s], 0)
        add_outer(illum, whole[:tile], s)
        add_inner(illum, whole[tile:], s)
        return carry

    def relay(c):
        @pl.when(has_far)
        def _():
            forward_near(c).wait_recv()
            for j in range(nm - 1):
                spread(far_blk, c, j, brf_s, brf_r).start()

    for c in range(chunks - 1):
        relay(c)
    lax.fori_loop(0, slots, add_illum, 0)
    relay(chunks - 1)

    def illum_far():
        return remote(
            illum.at[rows_of(far_blk, m), :], il_far_in, ilf_s.at[0], ilf_r.at[0], far_dev, m
        )

    def illum_near():
        return remote(il_near_out, il_near_in, iln_s.at[0], iln_r.at[0], near_dev, m)

    @pl.when(has_far)
    def _():
        illum_far().start()

    for c in range(chunks):
        for j in range(nm - 1):
            spread(near_blk, c, j, brn_s, brn_r).wait_recv()

    @pl.when(has_far)
    def _():
        for c in range(chunks):
            for j in range(nm - 1):
                spread(far_blk, c, j, brf_s, brf_r).wait_recv()

    def power_copy(s, j):
        return remote(
            power.at[s], power_in.at[s, j], pow_s.at[s, j], pow_r.at[s, j], p, others[j]
        )

    def forward(s, carry):
        below = line < row_ref[s]
        win_re, win_im = (
            narrowed(jnp.where(below, ext[i, 2 * tile :, :], ext[i, :tile, :]), s) for i in (0, 1)
        )
        for k in range(modes):
            half = early[s, k] + exits(s, k, 0, win_re, win_im)
            half = half.astype(bf16)
            stage[k * pat : (k + 1) * pat, :pat] = half[:pat]
            stage[k * pat : (k + 1) * pat, pat:] = half[pat:]
        wave_ref[s] = jnp.dot(stage[...], turned_ref[...], preferred_element_type=f32)
        model = jnp.zeros((pat, pat), f32)
        for k in range(modes):
            wave = wave_ref[s, k * pat : (k + 1) * pat, :]
            model = model + wave[:, :pat] * wave[:, :pat] + wave[:, pat:] * wave[:, pat:]
        power[s] = model
        for j in range(nm - 1):
            power_copy(s, j).start()
        return carry

    lax.fori_loop(0, slots, forward, 0)

    @pl.when(has_back)
    def _():
        illum_far().wait_recv()
        il_near_out[...] = illum[rows_of(near_blk, m), :] + il_far_in[...]

    @pl.when(jnp.logical_not(has_back))
    def _():
        il_near_out[...] = illum[rows_of(near_blk, m), :]

    illum_near().start()

    def numerators(s, part):
        for k in range(modes):
            back = jnp.dot(right[s, part], fixed_ref[s, k], preferred_element_type=f32)
            back = back.astype(bf16)
            stage[k * tile : (k + 1) * tile, :pat] = back[:tile]
            stage[k * tile : (k + 1) * tile, pat:] = back[tile:]
        delta_ref[...] = jnp.dot(
            stage[: modes * tile, :], plain_ref[...], preferred_element_type=f32
        )
        numer_re = jnp.zeros((tile, pat), f32)
        numer_im = jnp.zeros((tile, pat), f32)
        rows = slice(part * tile, (part + 1) * tile)
        for k in range(modes):
            delta = delta_ref[k * tile : (k + 1) * tile, :]
            delta_re = delta[:, :pat] - exit_ref[s, k, part, :tile, :].astype(f32)
            delta_im = delta[:, pat:] - exit_ref[s, k, part, tile:, :].astype(f32)
            probe_re, probe_im = spun[s, 0, k, rows, :], spun[s, 1, k, rows, :]
            numer_re = numer_re + probe_re * delta_re + probe_im * delta_im
            numer_im = numer_im + probe_re * delta_im - probe_im * delta_re
        on = s < live
        return jnp.where(on, numer_re, 0.0), jnp.where(on, numer_im, 0.0)

    def backward_outer(s, carry):
        model = power[s]
        for j in range(nm - 1):
            power_copy(s, j).wait_recv()
            model = model + power_in[s, j]
        scaling = jnp.sqrt(meas_ref[s]) / jnp.maximum(jnp.sqrt(model), 1.0)
        for k in range(modes):
            block = slice(k * pat, (k + 1) * pat)
            fixed_ref[s, k, :pat, :] = (scaling * wave_ref[s, block, :pat]).astype(bf16)
            fixed_ref[s, k, pat:, :] = (scaling * wave_ref[s, block, pat:]).astype(bf16)
        for i, numer in enumerate(numerators(s, 0)):
            add_outer(acc.at[i], numer, s)
        return carry

    def backward_inner(s, carry):
        for i, numer in enumerate(numerators(s, 1)):
            add_inner(acc.at[i], numer, s)
        return carry

    lax.fori_loop(0, slots, backward_outer, 0)

    blocks = (far_blk, near_blk, 1)

    def reduce_copy(b, j):
        return remote(
            acc.at[:, rows_of(blocks[b], others[j]), :], red_in.at[j, b],
            red_s.at[j, b], red_r.at[j, b], p, others[j],
        )

    for b in (0, 1):
        for j in range(nm - 1):
            reduce_copy(b, j).start()

    def reduced(b):
        value = acc[:, rows_of(blocks[b], m), :]
        for j in range(nm - 1):
            reduce_copy(b, j).wait_recv()
            value = value + red_in[j, b]
        return value

    def far_copy(c):
        part = pl.ds(c * piece, piece)
        return remote(
            far_out.at[:, part, :], far_in.at[:, part, :], rf_s.at[c], rf_r.at[c], far_dev, m
        )

    def near_copy(c):
        part = pl.ds(c * piece, piece)
        return remote(
            near_out.at[:, part, :], near_in.at[:, part, :], rn_s.at[c], rn_r.at[c], near_dev, m
        )

    first = slots // 3
    second = slots - slots // 3
    lax.fori_loop(0, first, backward_inner, 0)
    far_out[...] = reduced(0)

    @pl.when(has_far)
    def _():
        for c in range(chunks):
            far_copy(c).start()

    near_out[...] = reduced(1)

    def pass_on(c):
        @pl.when(has_back)
        def _():
            part = pl.ds(c * piece, piece)
            far_copy(c).wait_recv()
            near_out[:, part, :] = near_out[:, part, :] + far_in[:, part, :]

        near_copy(c).start()

    lax.fori_loop(first, second, backward_inner, 0)
    pass_on(0)
    lax.fori_loop(second, slots, backward_inner, 0)
    for j in range(nm - 1):
        reduce_copy(2, j).start()
    for c in range(1, chunks):
        pass_on(c)

    own_sum = reduced(2)
    illum_near().wait_recv()
    weight = 1.0 / (illum[rows_of(1, m), :] + il_near_in[...] + 1.0)
    for c in range(chunks):
        near_copy(c).wait_recv()
        part = slice(c * piece, (c + 1) * piece)
        out_ref[:, part, :] = ext[:, rows_of(1, m, c, piece), :] + (
            own_sum[:, part] + near_in[:, part, :]
        ) * weight[part]

    for c in range(chunks):
        halo(c).wait_send()
        near_copy(c).wait_send()
        for j in range(nm - 1):
            spread(near_blk, c, j, brn_s, brn_r).wait_send()
    for j in range(nm - 1):
        pp_copy(j).wait_send()
        for s in range(slots):
            power_copy(s, j).wait_send()
        for b in range(3):
            reduce_copy(b, j).wait_send()
    illum_near().wait_send()

    @pl.when(has_far)
    def _():
        illum_far().wait_send()
        for c in range(chunks):
            far_copy(c).wait_send()
            for j in range(nm - 1):
                spread(far_blk, c, j, brf_s, brf_r).wait_send()

    @pl.when(has_back)
    def _():
        for c in range(chunks):
            forward_near(c).wait_send()


def local(object_field, probe, measured, row_offsets, col_offsets, tile_counts):
    n, nm = lax.axis_size("pos"), lax.axis_size("mode")
    tile, cols = object_field.shape[1:]
    slots, pat = measured.shape[:2]
    modes = probe.shape[1]
    share = tile // nm
    chunks = min(4, share // 8)
    f32, bf16 = jnp.float32, jnp.bfloat16
    vmem = pl.BlockSpec(memory_space=pltpu.VMEM)
    anywhere = pl.BlockSpec(memory_space=pltpu.HBM)
    dma = pltpu.SemaphoreType.DMA
    others = nm - 1
    scratch = [
        pltpu.SMEM((slots,), jnp.int32),
        pltpu.SMEM((slots,), jnp.int32),
        pltpu.SMEM((1,), jnp.int32),
        pltpu.VMEM((2, modes, pat, pat), f32),
        pltpu.VMEM((slots, pat, pat), f32),
        pltpu.VMEM((2 * pat, 2 * pat), bf16),
        pltpu.VMEM((2 * pat, 2 * pat), bf16),
        dma((6,)),
        pltpu.VMEM((2, pat, pat), f32),
        pltpu.VMEM((slots, 2, 2 * pat, pat), bf16),
        pltpu.VMEM((slots, 2, pat, 2 * pat), bf16),
        pltpu.VMEM((slots, modes, 2 * pat, pat), bf16),
        pltpu.VMEM((slots, 2, modes, pat, pat), f32),
        pltpu.VMEM((slots, modes, 2 * pat, pat), f32),
        pltpu.VMEM((modes * pat, 2 * pat), bf16),
        pltpu.VMEM((modes * tile, 2 * pat), f32),
        pltpu.VMEM((2, 3 * tile, cols), f32),
        pltpu.VMEM((2, 3 * tile, cols), f32),
        pltpu.VMEM((3 * tile, cols), f32),
        pltpu.VMEM((slots, modes, 2, pat, pat), bf16),
        pltpu.VMEM((slots, modes * pat, 2 * pat), f32),
        pltpu.VMEM((slots, pat, pat), f32),
        pltpu.VMEM((slots, others, pat, pat), f32),
        pltpu.VMEM((pat, pat), f32),
        pltpu.VMEM((others, pat, pat), f32),
        pltpu.VMEM((others, 3, 2, share, cols), f32),
        pltpu.VMEM((2, share, cols), f32),
        pltpu.VMEM((2, share, cols), f32),
        pltpu.VMEM((2, share, cols), f32),
        pltpu.VMEM((2, share, cols), f32),
        pltpu.VMEM((share, cols), f32),
        pltpu.VMEM((share, cols), f32),
        pltpu.VMEM((share, cols), f32),
        dma((chunks,)), dma((chunks,)), dma((chunks,)), dma((chunks,)),
        dma((others, chunks)), dma((others, chunks)), dma((others, chunks)), dma((others, chunks)),
        dma((slots, others)), dma((slots, others)), dma((others,)), dma((others,)),
        dma((1,)), dma((1,)), dma((1,)), dma((1,)),
        dma((others, 3)), dma((others, 3)),
        dma((chunks,)), dma((chunks,)), dma((chunks,)), dma((chunks,)),
    ]
    return pl.pallas_call(
        functools.partial(kernel, n, nm, chunks),
        out_shape=jax.ShapeDtypeStruct((2, share, cols), f32),
        in_specs=[anywhere] * 6,
        out_specs=vmem,
        scratch_shapes=scratch,
        compiler_params=pltpu.CompilerParams(
            collective_id=0, has_side_effects=True, vmem_limit_bytes=64 * 1024 * 1024
        ),
    )(
        row_offsets, col_offsets, tile_counts, object_field, probe, measured
    )


def solution(mesh):
    in_specs = (
        P(None, "pos", None),
        P(None, "mode", None, None),
        P("pos", None, None),
        P("pos"),
        P("pos"),
        P("pos"),
    )
    out_specs = P(None, ("pos", "mode"), None)
    return jax.shard_map(local, mesh=mesh, in_specs=in_specs, out_specs=out_specs, check_vma=False)
```

```python
import functools
import math

import jax
import jax.numpy as jnp
from jax import lax
from jax.experimental import pallas as pl
from jax.experimental.pallas import tpu as pltpu
from jax.sharding import PartitionSpec as P

MESH = pl.DeviceIdType.MESH


def sine_of(step, period):
    step = jnp.bitwise_and(step, period - 1)
    step = jnp.where(step >= period // 2, step - period, step)
    step = jnp.where(step > period // 4, period // 2 - step, step)
    step = jnp.where(step < -(period // 4), -(period // 2) - step, step)
    x = step.astype(jnp.float32) * (2.0 * math.pi / period)
    y = x * x
    total = jnp.full_like(x, -1.0 / math.factorial(11))
    for order in (9, 7, 5, 3, 1):
        total = total * y + (-1.0) ** (order // 2) / math.factorial(order)
    return x * total


def dft_tables(pattern):
    rows = lax.broadcasted_iota(jnp.int32, (pattern, pattern), 0)
    columns = lax.broadcasted_iota(jnp.int32, (pattern, pattern), 1)
    phases = rows * columns
    factor = 1.0 / math.sqrt(pattern)
    real = sine_of(phases + pattern // 4, pattern) * factor
    imag = -sine_of(phases, pattern) * factor
    return real, imag


def kernel(
    n, nm, chunks,
    row_hbm, col_hbm, count_hbm, obj_hbm, probe_hbm, meas_hbm,
    out_ref,
    row_ref, col_ref, count_ref, probe_ref, meas_ref, plain_ref, turned_ref, load_s,
    base, left, right, fixed_ref, spun, early, stage, delta_ref, ext, acc, illum, exit_ref, wave_ref, power, power_in, pp, pp_in, red_in,
    far_out, far_in, near_out, near_in, il_far_in, il_near_out, il_near_in,
    halo_s, halo_r, fwd_s, fwd_r, brn_s, brn_r, brf_s, brf_r,
    pow_s, pow_r, pp_s, pp_r, ilf_s, ilf_r, iln_s, iln_r,
    red_s, red_r, rf_s, rf_r, rn_s, rn_r,
):
    tile, cols = obj_hbm.shape[1], obj_hbm.shape[2]
    slots, pat = meas_ref.shape[0], meas_ref.shape[1]
    modes = probe_ref.shape[1]
    share = tile // nm
    piece = share // chunks
    assert pat == 2 * tile
    f32, bf16 = jnp.float32, jnp.bfloat16

    p = lax.axis_index("pos")
    m = lax.axis_index("mode")
    odd = lax.rem(p, 2)
    near_dev = p + 1 - 2 * odd
    far_blk = 2 * odd
    near_blk = 2 - far_blk
    far_raw = p - 2 + 4 * odd
    back_raw = p + 2 - 4 * odd
    has_far = jnp.logical_and(far_raw >= 0, far_raw < n)
    has_back = jnp.logical_and(back_raw >= 0, back_raw < n)
    far_dev = lax.rem(far_raw + n, n)
    back_dev = lax.rem(back_raw + n, n)
    others = [lax.rem(m + j, nm) for j in range(1, nm)]

    def rows_of(block, mode, c=0, size=None):
        size = share if size is None else size
        return pl.ds(pl.multiple_of(block * tile + mode * share + c * piece, 8), size)

    def remote(src, dst, s, r, pos, mode):
        return pltpu.make_async_remote_copy(
            src_ref=src, dst_ref=dst, send_sem=s, recv_sem=r,
            device_id=(pos, mode), device_id_type=MESH,
        )

    own = ext.at[:, tile : 2 * tile, :]
    pairs = (
        (probe_hbm, probe_ref), (row_hbm, row_ref), (col_hbm, col_ref), (count_hbm, count_ref),
        (obj_hbm, own), (meas_hbm, meas_ref),
    )
    loads = [pltpu.make_async_copy(a, b, load_s.at[i]) for i, (a, b) in enumerate(pairs)]
    def fill(table, real, imag, sign):
        high, wide = table.shape[0] // 2, table.shape[1] // 2
        real = real.astype(jnp.bfloat16)
        table[:high, :wide] = real
        table[high:, wide:] = real
        table[:high, wide:] = (sign * imag).astype(jnp.bfloat16)
        table[high:, :wide] = (-sign * imag).astype(jnp.bfloat16)

    barrier = pltpu.get_barrier_semaphore()
    pl.semaphore_signal(barrier, inc=1, device_id=(near_dev, m), device_id_type=MESH)
    for other in others:
        pl.semaphore_signal(barrier, inc=1, device_id=(p, other), device_id_type=MESH)

    @pl.when(has_far)
    def _():
        pl.semaphore_signal(barrier, inc=1, device_id=(far_dev, m), device_id_type=MESH)

    @pl.when(has_back)
    def _():
        pl.semaphore_signal(barrier, inc=1, device_id=(back_dev, m), device_id_type=MESH)

    greeted = has_far.astype(jnp.int32) + has_back.astype(jnp.int32)
    for load in loads:
        load.start()
    real, imag = dft_tables(pat)
    base[0] = real
    base[1] = imag
    for table, sign in ((plain_ref, -1.0), (turned_ref, 1.0)):
        fill(table, real, imag, sign)
    pl.semaphore_wait(barrier, nm + greeted)

    def halo(c):
        return remote(
            obj_hbm.at[:, rows_of(0, m, c, piece), :], ext.at[:, rows_of(far_blk, m, c, piece), :],
            halo_s.at[c], halo_r.at[c], near_dev, m,
        )

    def forward_near(c):
        return remote(
            ext.at[:, rows_of(near_blk, m, c, piece), :],
            ext.at[:, rows_of(far_blk, m, c, piece), :],
            fwd_s.at[c], fwd_r.at[c], back_dev, m,
        )

    def spread(block, c, j, s, r):
        where = rows_of(block, m, c, piece)
        return remote(
            ext.at[:, where, :], ext.at[:, where, :], s.at[j, c], r.at[j, c], p, others[j]
        )

    for c in range(chunks):
        halo(c).start()

    loads[0].wait()
    total = jnp.zeros((pat, pat), jnp.float32)
    for k in range(modes):
        total = total + probe_ref[0, k] * probe_ref[0, k] + probe_ref[1, k] * probe_ref[1, k]
    pp[...] = total

    def pp_copy(j):
        return remote(pp, pp_in.at[j], pp_s.at[j], pp_r.at[j], p, others[j])

    for j in range(nm - 1):
        pp_copy(j).start()

    for load in loads[1:]:
        load.wait()
    acc[...] = jnp.zeros_like(acc)
    illum[...] = jnp.zeros_like(illum)

    @pl.when(jnp.logical_not(has_far))
    def _():
        ext[:, pl.ds(pl.multiple_of(far_blk * tile, 8), tile), :] = jnp.zeros(
            (2, tile, cols), jnp.float32
        )

    line = lax.broadcasted_iota(jnp.int32, (tile, cols), 0)

    def narrowed(rows, slot):
        return pltpu.roll(rows, lax.rem(cols - col_ref[slot], cols), 1)[:, :pat]

    def widened(values, slot):
        blank = jnp.zeros((tile, cols - pat), f32)
        return pltpu.roll(jnp.concatenate([values, blank], axis=1), col_ref[slot], 1)

    def add_outer(total, values, slot):
        wide, below = widened(values, slot), line < row_ref[slot]
        total[:tile, :] += jnp.where(below, 0.0, wide)
        total[2 * tile :, :] += jnp.where(below, wide, 0.0)

    def add_inner(total, values, slot):
        total[tile : 2 * tile, :] += widened(values, slot)

    def exits(s, k, part, win_re, win_im):
        rows = slice(part * tile, (part + 1) * tile)
        probe_re, probe_im = spun[s, 0, k, rows, :], spun[s, 1, k, rows, :]
        exit_re = (probe_re * win_re - probe_im * win_im).astype(bf16)
        exit_im = (probe_re * win_im + probe_im * win_re).astype(bf16)
        stacked = jnp.concatenate([exit_re, exit_im], axis=0)
        exit_ref[s, k, part] = stacked
        return jnp.dot(left[s, part], stacked, preferred_element_type=f32)

    def turn_tables(s):
        shift = row_ref[s]
        real, imag = (pltpu.roll(base[i], shift, 1) for i in (0, 1))
        for part in (0, 1):
            columns = slice(part * tile, (part + 1) * tile)
            fill(left.at[s, part], real[:, columns], imag[:, columns], -1.0)
        real, imag = (pltpu.roll(base[i], shift, 0) for i in (0, 1))
        for part in (0, 1):
            rows = slice(part * tile, (part + 1) * tile)
            fill(right.at[s, part], real[rows], imag[rows], 1.0)

    def turn_probes(s):
        for i in (0, 1):
            for k in range(modes):
                spun[s, i, k] = pltpu.roll(probe_ref[i, k], row_ref[s], 0)

    def start_products(s):
        win_re = narrowed(ext[0, tile : 2 * tile, :], s)
        win_im = narrowed(ext[1, tile : 2 * tile, :], s)
        for k in range(modes):
            early[s, k] = exits(s, k, 1, win_re, win_im)

    work = [
        functools.partial(do, s)
        for s in range(slots)
        for do in (turn_tables, turn_probes, start_products)
    ]

    for c in range(max(chunks, len(work))):
        if c < len(work):
            work[c]()
        if c >= chunks:
            continue
        halo(c).wait_recv()

        @pl.when(has_back)
        def _():
            forward_near(c).start()

        for j in range(nm - 1):
            spread(near_blk, c, j, brn_s, brn_r).start()

    for j in range(nm - 1):
        pp_copy(j).wait_recv()

    live = count_ref[0]

    def add_illum(s, carry):
        whole = pp[...]
        for j in range(nm - 1):
            whole = whole + pp_in[j]
        whole = jnp.where(s < live, whole, 0.0)
        whole = pltpu.roll(whole, row_ref[s], 0)
        add_outer(illum, whole[:tile], s)
        add_inner(illum, whole[tile:], s)
        return carry

    def relay(c):
        @pl.when(has_far)
        def _():
            forward_near(c).wait_recv()
            for j in range(nm - 1):
                spread(far_blk, c, j, brf_s, brf_r).start()

    for c in range(chunks - 1):
        relay(c)
    lax.fori_loop(0, slots, add_illum, 0)
    relay(chunks - 1)

    def illum_far():
        return remote(
            illum.at[rows_of(far_blk, m), :], il_far_in, ilf_s.at[0], ilf_r.at[0], far_dev, m
        )

    def illum_near():
        return remote(il_near_out, il_near_in, iln_s.at[0], iln_r.at[0], near_dev, m)

    @pl.when(has_far)
    def _():
        illum_far().start()

    for c in range(chunks):
        for j in range(nm - 1):
            spread(near_blk, c, j, brn_s, brn_r).wait_recv()

    @pl.when(has_far)
    def _():
        for c in range(chunks):
            for j in range(nm - 1):
                spread(far_blk, c, j, brf_s, brf_r).wait_recv()

    def power_copy(s, j):
        return remote(
            power.at[s], power_in.at[s, j], pow_s.at[s, j], pow_r.at[s, j], p, others[j]
        )

    def forward(s, carry):
        below = line < row_ref[s]
        win_re, win_im = (
            narrowed(jnp.where(below, ext[i, 2 * tile :, :], ext[i, :tile, :]), s) for i in (0, 1)
        )
        for k in range(modes):
            half = early[s, k] + exits(s, k, 0, win_re, win_im)
            half = half.astype(bf16)
            stage[k * pat : (k + 1) * pat, :pat] = half[:pat]
            stage[k * pat : (k + 1) * pat, pat:] = half[pat:]
        wave_ref[s] = jnp.dot(stage[...], turned_ref[...], preferred_element_type=f32)
        model = jnp.zeros((pat, pat), f32)
        for k in range(modes):
            wave = wave_ref[s, k * pat : (k + 1) * pat, :]
            model = model + wave[:, :pat] * wave[:, :pat] + wave[:, pat:] * wave[:, pat:]
        power[s] = model
        for j in range(nm - 1):
            power_copy(s, j).start()
        return carry

    lax.fori_loop(0, slots, forward, 0)

    @pl.when(has_back)
    def _():
        illum_far().wait_recv()
        il_near_out[...] = illum[rows_of(near_blk, m), :] + il_far_in[...]

    @pl.when(jnp.logical_not(has_back))
    def _():
        il_near_out[...] = illum[rows_of(near_blk, m), :]

    illum_near().start()

    def numerators(s, part):
        for k in range(modes):
            back = jnp.dot(right[s, part], fixed_ref[s, k], preferred_element_type=f32)
            back = back.astype(bf16)
            stage[k * tile : (k + 1) * tile, :pat] = back[:tile]
            stage[k * tile : (k + 1) * tile, pat:] = back[tile:]
        delta_ref[...] = jnp.dot(
            stage[: modes * tile, :], plain_ref[...], preferred_element_type=f32
        )
        numer_re = jnp.zeros((tile, pat), f32)
        numer_im = jnp.zeros((tile, pat), f32)
        rows = slice(part * tile, (part + 1) * tile)
        for k in range(modes):
            delta = delta_ref[k * tile : (k + 1) * tile, :]
            delta_re = delta[:, :pat] - exit_ref[s, k, part, :tile, :].astype(f32)
            delta_im = delta[:, pat:] - exit_ref[s, k, part, tile:, :].astype(f32)
            probe_re, probe_im = spun[s, 0, k, rows, :], spun[s, 1, k, rows, :]
            numer_re = numer_re + probe_re * delta_re + probe_im * delta_im
            numer_im = numer_im + probe_re * delta_im - probe_im * delta_re
        on = s < live
        return jnp.where(on, numer_re, 0.0), jnp.where(on, numer_im, 0.0)

    def backward_outer(s, carry):
        model = power[s]
        for j in range(nm - 1):
            power_copy(s, j).wait_recv()
            model = model + power_in[s, j]
        scaling = jnp.sqrt(meas_ref[s]) / jnp.maximum(jnp.sqrt(model), 1.0)
        for k in range(modes):
            block = slice(k * pat, (k + 1) * pat)
            fixed_ref[s, k, :pat, :] = (scaling * wave_ref[s, block, :pat]).astype(bf16)
            fixed_ref[s, k, pat:, :] = (scaling * wave_ref[s, block, pat:]).astype(bf16)
        for i, numer in enumerate(numerators(s, 0)):
            add_outer(acc.at[i], numer, s)
        return carry

    def backward_inner(s, carry):
        for i, numer in enumerate(numerators(s, 1)):
            add_inner(acc.at[i], numer, s)
        return carry

    lax.fori_loop(0, slots, backward_outer, 0)

    blocks = (far_blk, near_blk, 1)

    def reduce_copy(b, j):
        return remote(
            acc.at[:, rows_of(blocks[b], others[j]), :], red_in.at[j, b],
            red_s.at[j, b], red_r.at[j, b], p, others[j],
        )

    for b in (0, 1):
        for j in range(nm - 1):
            reduce_copy(b, j).start()

    def reduced(b):
        value = acc[:, rows_of(blocks[b], m), :]
        for j in range(nm - 1):
            reduce_copy(b, j).wait_recv()
            value = value + red_in[j, b]
        return value

    def far_copy(c):
        part = pl.ds(c * piece, piece)
        return remote(
            far_out.at[:, part, :], far_in.at[:, part, :], rf_s.at[c], rf_r.at[c], far_dev, m
        )

    def near_copy(c):
        part = pl.ds(c * piece, piece)
        return remote(
            near_out.at[:, part, :], near_in.at[:, part, :], rn_s.at[c], rn_r.at[c], near_dev, m
        )

    first = slots // 3
    second = slots - slots // 3
    lax.fori_loop(0, first, backward_inner, 0)
    far_out[...] = reduced(0)

    @pl.when(has_far)
    def _():
        for c in range(chunks):
            far_copy(c).start()

    near_out[...] = reduced(1)

    def pass_on(c):
        @pl.when(has_back)
        def _():
            part = pl.ds(c * piece, piece)
            far_copy(c).wait_recv()
            near_out[:, part, :] = near_out[:, part, :] + far_in[:, part, :]

        near_copy(c).start()

    lax.fori_loop(first, second, backward_inner, 0)
    pass_on(0)
    lax.fori_loop(second, slots, backward_inner, 0)
    for j in range(nm - 1):
        reduce_copy(2, j).start()
    for c in range(1, chunks):
        pass_on(c)

    own_sum = reduced(2)
    illum_near().wait_recv()
    weight = 1.0 / (illum[rows_of(1, m), :] + il_near_in[...] + 1.0)
    for c in range(chunks):
        near_copy(c).wait_recv()
        part = slice(c * piece, (c + 1) * piece)
        out_ref[:, part, :] = ext[:, rows_of(1, m, c, piece), :] + (
            own_sum[:, part] + near_in[:, part, :]
        ) * weight[part]

    for c in range(chunks):
        halo(c).wait_send()
        near_copy(c).wait_send()
        for j in range(nm - 1):
            spread(near_blk, c, j, brn_s, brn_r).wait_send()
    for j in range(nm - 1):
        pp_copy(j).wait_send()
        for s in range(slots):
            power_copy(s, j).wait_send()
        for b in range(3):
            reduce_copy(b, j).wait_send()
    illum_near().wait_send()

    @pl.when(has_far)
    def _():
        illum_far().wait_send()
        for c in range(chunks):
            far_copy(c).wait_send()
            for j in range(nm - 1):
                spread(far_blk, c, j, brf_s, brf_r).wait_send()

    @pl.when(has_back)
    def _():
        for c in range(chunks):
            forward_near(c).wait_send()


def local(object_field, probe, measured, row_offsets, col_offsets, tile_counts):
    n, nm = lax.axis_size("pos"), lax.axis_size("mode")
    tile, cols = object_field.shape[1:]
    slots, pat = measured.shape[:2]
    modes = probe.shape[1]
    share = tile // nm
    chunks = min(8, share // 8)
    f32, bf16 = jnp.float32, jnp.bfloat16
    vmem = pl.BlockSpec(memory_space=pltpu.VMEM)
    anywhere = pl.BlockSpec(memory_space=pltpu.HBM)
    dma = pltpu.SemaphoreType.DMA
    others = nm - 1
    scratch = [
        pltpu.SMEM((slots,), jnp.int32),
        pltpu.SMEM((slots,), jnp.int32),
        pltpu.SMEM((1,), jnp.int32),
        pltpu.VMEM((2, modes, pat, pat), f32),
        pltpu.VMEM((slots, pat, pat), f32),
        pltpu.VMEM((2 * pat, 2 * pat), bf16),
        pltpu.VMEM((2 * pat, 2 * pat), bf16),
        dma((6,)),
        pltpu.VMEM((2, pat, pat), f32),
        pltpu.VMEM((slots, 2, 2 * pat, pat), bf16),
        pltpu.VMEM((slots, 2, pat, 2 * pat), bf16),
        pltpu.VMEM((slots, modes, 2 * pat, pat), bf16),
        pltpu.VMEM((slots, 2, modes, pat, pat), f32),
        pltpu.VMEM((slots, modes, 2 * pat, pat), f32),
        pltpu.VMEM((modes * pat, 2 * pat), bf16),
        pltpu.VMEM((modes * tile, 2 * pat), f32),
        pltpu.VMEM((2, 3 * tile, cols), f32),
        pltpu.VMEM((2, 3 * tile, cols), f32),
        pltpu.VMEM((3 * tile, cols), f32),
        pltpu.VMEM((slots, modes, 2, pat, pat), bf16),
        pltpu.VMEM((slots, modes * pat, 2 * pat), f32),
        pltpu.VMEM((slots, pat, pat), f32),
        pltpu.VMEM((slots, others, pat, pat), f32),
        pltpu.VMEM((pat, pat), f32),
        pltpu.VMEM((others, pat, pat), f32),
        pltpu.VMEM((others, 3, 2, share, cols), f32),
        pltpu.VMEM((2, share, cols), f32),
        pltpu.VMEM((2, share, cols), f32),
        pltpu.VMEM((2, share, cols), f32),
        pltpu.VMEM((2, share, cols), f32),
        pltpu.VMEM((share, cols), f32),
        pltpu.VMEM((share, cols), f32),
        pltpu.VMEM((share, cols), f32),
        dma((chunks,)), dma((chunks,)), dma((chunks,)), dma((chunks,)),
        dma((others, chunks)), dma((others, chunks)), dma((others, chunks)), dma((others, chunks)),
        dma((slots, others)), dma((slots, others)), dma((others,)), dma((others,)),
        dma((1,)), dma((1,)), dma((1,)), dma((1,)),
        dma((others, 3)), dma((others, 3)),
        dma((chunks,)), dma((chunks,)), dma((chunks,)), dma((chunks,)),
    ]
    return pl.pallas_call(
        functools.partial(kernel, n, nm, chunks),
        out_shape=jax.ShapeDtypeStruct((2, share, cols), f32),
        in_specs=[anywhere] * 6,
        out_specs=vmem,
        scratch_shapes=scratch,
        compiler_params=pltpu.CompilerParams(
            collective_id=0, has_side_effects=True, vmem_limit_bytes=64 * 1024 * 1024
        ),
    )(
        row_offsets, col_offsets, tile_counts, object_field, probe, measured
    )


def solution(mesh):
    in_specs = (
        P(None, "pos", None),
        P(None, "mode", None, None),
        P("pos", None, None),
        P("pos"),
        P("pos"),
        P("pos"),
    )
    out_specs = P(None, ("pos", "mode"), None)
    return jax.shard_map(local, mesh=mesh, in_specs=in_specs, out_specs=out_specs, check_vma=False)
```

```python
import functools
import math

import jax
import jax.numpy as jnp
from jax import lax
from jax.experimental import pallas as pl
from jax.experimental.pallas import tpu as pltpu
from jax.sharding import PartitionSpec as P

MESH = pl.DeviceIdType.MESH


def sine_of(step, period):
    step = jnp.bitwise_and(step, period - 1)
    step = jnp.where(step >= period // 2, step - period, step)
    step = jnp.where(step > period // 4, period // 2 - step, step)
    step = jnp.where(step < -(period // 4), -(period // 2) - step, step)
    x = step.astype(jnp.float32) * (2.0 * math.pi / period)
    y = x * x
    total = jnp.full_like(x, -1.0 / math.factorial(11))
    for order in (9, 7, 5, 3, 1):
        total = total * y + (-1.0) ** (order // 2) / math.factorial(order)
    return x * total


def dft_tables(pattern):
    rows = lax.broadcasted_iota(jnp.int32, (pattern, pattern), 0)
    columns = lax.broadcasted_iota(jnp.int32, (pattern, pattern), 1)
    phases = rows * columns
    factor = 1.0 / math.sqrt(pattern)
    real = sine_of(phases + pattern // 4, pattern) * factor
    imag = -sine_of(phases, pattern) * factor
    return real, imag


def kernel(
    n, nm, chunks,
    row_hbm, col_hbm, count_hbm, obj_hbm, probe_hbm, meas_hbm,
    out_ref,
    row_ref, col_ref, count_ref, probe_ref, meas_ref, plain_ref, turned_ref, load_s,
    base, left, right, fixed_ref, spun, early, stage, delta_ref, ext, acc, illum, exit_ref, wave_ref, power, power_in, pp, pp_in, red_in,
    far_out, far_in, near_out, near_in, il_far_in, il_near_out, il_near_in,
    halo_s, halo_r, fwd_s, fwd_r, brn_s, brn_r, brf_s, brf_r,
    pow_s, pow_r, pp_s, pp_r, ilf_s, ilf_r, iln_s, iln_r,
    red_s, red_r, rf_s, rf_r, rn_s, rn_r,
):
    tile, cols = obj_hbm.shape[1], obj_hbm.shape[2]
    slots, pat = meas_ref.shape[0], meas_ref.shape[1]
    modes = probe_ref.shape[1]
    share = tile // nm
    piece = share // chunks
    assert pat == 2 * tile
    f32, bf16 = jnp.float32, jnp.bfloat16

    p = lax.axis_index("pos")
    m = lax.axis_index("mode")
    odd = lax.rem(p, 2)
    near_dev = p + 1 - 2 * odd
    far_blk = 2 * odd
    near_blk = 2 - far_blk
    far_raw = p - 2 + 4 * odd
    back_raw = p + 2 - 4 * odd
    has_far = jnp.logical_and(far_raw >= 0, far_raw < n)
    has_back = jnp.logical_and(back_raw >= 0, back_raw < n)
    far_dev = lax.rem(far_raw + n, n)
    back_dev = lax.rem(back_raw + n, n)
    others = [lax.rem(m + j, nm) for j in range(1, nm)]

    def rows_of(block, mode, c=0, size=None):
        size = share if size is None else size
        return pl.ds(pl.multiple_of(block * tile + mode * share + c * piece, 8), size)

    def remote(src, dst, s, r, pos, mode):
        return pltpu.make_async_remote_copy(
            src_ref=src, dst_ref=dst, send_sem=s, recv_sem=r,
            device_id=(pos, mode), device_id_type=MESH,
        )

    own = ext.at[:, tile : 2 * tile, :]
    pairs = (
        (probe_hbm, probe_ref), (row_hbm, row_ref), (col_hbm, col_ref), (count_hbm, count_ref),
        (obj_hbm, own), (meas_hbm, meas_ref),
    )
    loads = [pltpu.make_async_copy(a, b, load_s.at[i]) for i, (a, b) in enumerate(pairs)]
    def fill(table, real, imag, sign):
        high, wide = table.shape[0] // 2, table.shape[1] // 2
        real = real.astype(jnp.bfloat16)
        table[:high, :wide] = real
        table[high:, wide:] = real
        table[:high, wide:] = (sign * imag).astype(jnp.bfloat16)
        table[high:, :wide] = (-sign * imag).astype(jnp.bfloat16)

    barrier = pltpu.get_barrier_semaphore()
    pl.semaphore_signal(barrier, inc=1, device_id=(near_dev, m), device_id_type=MESH)
    for other in others:
        pl.semaphore_signal(barrier, inc=1, device_id=(p, other), device_id_type=MESH)

    @pl.when(has_far)
    def _():
        pl.semaphore_signal(barrier, inc=1, device_id=(far_dev, m), device_id_type=MESH)

    @pl.when(has_back)
    def _():
        pl.semaphore_signal(barrier, inc=1, device_id=(back_dev, m), device_id_type=MESH)

    greeted = has_far.astype(jnp.int32) + has_back.astype(jnp.int32)
    for load in loads:
        load.start()
    real, imag = dft_tables(pat)
    base[0] = real
    base[1] = imag
    for table, sign in ((plain_ref, -1.0), (turned_ref, 1.0)):
        fill(table, real, imag, sign)
    pl.semaphore_wait(barrier, nm + greeted)

    def halo(c):
        return remote(
            obj_hbm.at[:, rows_of(0, m, c, piece), :], ext.at[:, rows_of(far_blk, m, c, piece), :],
            halo_s.at[c], halo_r.at[c], near_dev, m,
        )

    def forward_near(c):
        return remote(
            ext.at[:, rows_of(near_blk, m, c, piece), :],
            ext.at[:, rows_of(far_blk, m, c, piece), :],
            fwd_s.at[c], fwd_r.at[c], back_dev, m,
        )

    def spread(block, c, j, s, r):
        where = rows_of(block, m, c, piece)
        return remote(
            ext.at[:, where, :], ext.at[:, where, :], s.at[j, c], r.at[j, c], p, others[j]
        )

    for c in range(chunks):
        halo(c).start()

    loads[0].wait()
    total = jnp.zeros((pat, pat), jnp.float32)
    for k in range(modes):
        total = total + probe_ref[0, k] * probe_ref[0, k] + probe_ref[1, k] * probe_ref[1, k]
    pp[...] = total

    def pp_copy(j):
        return remote(pp, pp_in.at[j], pp_s.at[j], pp_r.at[j], p, others[j])

    for j in range(nm - 1):
        pp_copy(j).start()

    for load in loads[1:]:
        load.wait()
    acc[...] = jnp.zeros_like(acc)
    illum[...] = jnp.zeros_like(illum)

    @pl.when(jnp.logical_not(has_far))
    def _():
        ext[:, pl.ds(pl.multiple_of(far_blk * tile, 8), tile), :] = jnp.zeros(
            (2, tile, cols), jnp.float32
        )

    line = lax.broadcasted_iota(jnp.int32, (tile, cols), 0)

    def narrowed(rows, slot):
        return pltpu.roll(rows, lax.rem(cols - col_ref[slot], cols), 1)[:, :pat]

    def widened(values, slot):
        blank = jnp.zeros((tile, cols - pat), f32)
        return pltpu.roll(jnp.concatenate([values, blank], axis=1), col_ref[slot], 1)

    def add_outer(total, values, slot):
        wide, below = widened(values, slot), line < row_ref[slot]
        total[:tile, :] += jnp.where(below, 0.0, wide)
        total[2 * tile :, :] += jnp.where(below, wide, 0.0)

    def add_inner(total, values, slot):
        total[tile : 2 * tile, :] += widened(values, slot)

    def exits(s, k, part, win_re, win_im):
        rows = slice(part * tile, (part + 1) * tile)
        probe_re, probe_im = spun[s, 0, k, rows, :], spun[s, 1, k, rows, :]
        exit_re = (probe_re * win_re - probe_im * win_im).astype(bf16)
        exit_im = (probe_re * win_im + probe_im * win_re).astype(bf16)
        stacked = jnp.concatenate([exit_re, exit_im], axis=0)
        exit_ref[s, k, part] = stacked
        return jnp.dot(left[s, part], stacked, preferred_element_type=f32)

    def turn_tables(s):
        shift = row_ref[s]
        real, imag = (pltpu.roll(base[i], shift, 1) for i in (0, 1))
        for part in (0, 1):
            columns = slice(part * tile, (part + 1) * tile)
            fill(left.at[s, part], real[:, columns], imag[:, columns], -1.0)
        real, imag = (pltpu.roll(base[i], shift, 0) for i in (0, 1))
        for part in (0, 1):
            rows = slice(part * tile, (part + 1) * tile)
            fill(right.at[s, part], real[rows], imag[rows], 1.0)

    def turn_probes(s):
        for i in (0, 1):
            for k in range(modes):
                spun[s, i, k] = pltpu.roll(probe_ref[i, k], row_ref[s], 0)

    def start_products(s):
        win_re = narrowed(ext[0, tile : 2 * tile, :], s)
        win_im = narrowed(ext[1, tile : 2 * tile, :], s)
        for k in range(modes):
            early[s, k] = exits(s, k, 1, win_re, win_im)

    work = [
        functools.partial(do, s)
        for s in range(slots)
        for do in (turn_tables, turn_probes, start_products)
    ]

    for c in range(max(chunks, len(work))):
        if c < len(work):
            work[c]()
        if c >= chunks:
            continue
        halo(c).wait_recv()

        @pl.when(has_back)
        def _():
            forward_near(c).start()

        for j in range(nm - 1):
            spread(near_blk, c, j, brn_s, brn_r).start()

    for j in range(nm - 1):
        pp_copy(j).wait_recv()

    live = count_ref[0]

    def add_illum(s, carry):
        whole = pp[...]
        for j in range(nm - 1):
            whole = whole + pp_in[j]
        whole = jnp.where(s < live, whole, 0.0)
        whole = pltpu.roll(whole, row_ref[s], 0)
        add_outer(illum, whole[:tile], s)
        add_inner(illum, whole[tile:], s)
        return carry

    def relay(c):
        @pl.when(has_far)
        def _():
            forward_near(c).wait_recv()
            for j in range(nm - 1):
                spread(far_blk, c, j, brf_s, brf_r).start()

    for c in range(chunks):
        relay(c)
    lax.fori_loop(0, slots, add_illum, 0)

    def illum_far():
        return remote(
            illum.at[rows_of(far_blk, m), :], il_far_in, ilf_s.at[0], ilf_r.at[0], far_dev, m
        )

    def illum_near():
        return remote(il_near_out, il_near_in, iln_s.at[0], iln_r.at[0], near_dev, m)

    @pl.when(has_far)
    def _():
        illum_far().start()

    for c in range(chunks):
        for j in range(nm - 1):
            spread(near_blk, c, j, brn_s, brn_r).wait_recv()

    @pl.when(has_far)
    def _():
        for c in range(chunks):
            for j in range(nm - 1):
                spread(far_blk, c, j, brf_s, brf_r).wait_recv()

    def power_copy(s, j):
        return remote(
            power.at[s], power_in.at[s, j], pow_s.at[s, j], pow_r.at[s, j], p, others[j]
        )

    def forward(s, carry):
        below = line < row_ref[s]
        win_re, win_im = (
            narrowed(jnp.where(below, ext[i, 2 * tile :, :], ext[i, :tile, :]), s) for i in (0, 1)
        )
        for k in range(modes):
            half = early[s, k] + exits(s, k, 0, win_re, win_im)
            half = half.astype(bf16)
            stage[k * pat : (k + 1) * pat, :pat] = half[:pat]
            stage[k * pat : (k + 1) * pat, pat:] = half[pat:]
        wave_ref[s] = jnp.dot(stage[...], turned_ref[...], preferred_element_type=f32)
        model = jnp.zeros((pat, pat), f32)
        for k in range(modes):
            wave = wave_ref[s, k * pat : (k + 1) * pat, :]
            model = model + wave[:, :pat] * wave[:, :pat] + wave[:, pat:] * wave[:, pat:]
        power[s] = model
        for j in range(nm - 1):
            power_copy(s, j).start()
        return carry

    lax.fori_loop(0, slots, forward, 0)

    @pl.when(has_back)
    def _():
        illum_far().wait_recv()
        il_near_out[...] = illum[rows_of(near_blk, m), :] + il_far_in[...]

    @pl.when(jnp.logical_not(has_back))
    def _():
        il_near_out[...] = illum[rows_of(near_blk, m), :]

    illum_near().start()

    def numerators(s, part):
        for k in range(modes):
            back = jnp.dot(right[s, part], fixed_ref[s, k], preferred_element_type=f32)
            back = back.astype(bf16)
            stage[k * tile : (k + 1) * tile, :pat] = back[:tile]
            stage[k * tile : (k + 1) * tile, pat:] = back[tile:]
        delta_ref[...] = jnp.dot(
            stage[: modes * tile, :], plain_ref[...], preferred_element_type=f32
        )
        numer_re = jnp.zeros((tile, pat), f32)
        numer_im = jnp.zeros((tile, pat), f32)
        rows = slice(part * tile, (part + 1) * tile)
        for k in range(modes):
            delta = delta_ref[k * tile : (k + 1) * tile, :]
            delta_re = delta[:, :pat] - exit_ref[s, k, part, :tile, :].astype(f32)
            delta_im = delta[:, pat:] - exit_ref[s, k, part, tile:, :].astype(f32)
            probe_re, probe_im = spun[s, 0, k, rows, :], spun[s, 1, k, rows, :]
            numer_re = numer_re + probe_re * delta_re + probe_im * delta_im
            numer_im = numer_im + probe_re * delta_im - probe_im * delta_re
        on = s < live
        return jnp.where(on, numer_re, 0.0), jnp.where(on, numer_im, 0.0)

    def backward_outer(s, carry):
        model = power[s]
        for j in range(nm - 1):
            power_copy(s, j).wait_recv()
            model = model + power_in[s, j]
        scaling = jnp.sqrt(meas_ref[s]) / jnp.maximum(jnp.sqrt(model), 1.0)
        for k in range(modes):
            block = slice(k * pat, (k + 1) * pat)
            fixed_ref[s, k, :pat, :] = (scaling * wave_ref[s, block, :pat]).astype(bf16)
            fixed_ref[s, k, pat:, :] = (scaling * wave_ref[s, block, pat:]).astype(bf16)
        for i, numer in enumerate(numerators(s, 0)):
            add_outer(acc.at[i], numer, s)
        return carry

    def backward_inner(s, carry):
        for i, numer in enumerate(numerators(s, 1)):
            add_inner(acc.at[i], numer, s)
        return carry

    lax.fori_loop(0, slots, backward_outer, 0)

    blocks = (far_blk, near_blk, 1)

    def reduce_copy(b, j):
        return remote(
            acc.at[:, rows_of(blocks[b], others[j]), :], red_in.at[j, b],
            red_s.at[j, b], red_r.at[j, b], p, others[j],
        )

    for b in (0, 1):
        for j in range(nm - 1):
            reduce_copy(b, j).start()

    def reduced(b):
        value = acc[:, rows_of(blocks[b], m), :]
        for j in range(nm - 1):
            reduce_copy(b, j).wait_recv()
            value = value + red_in[j, b]
        return value

    def far_copy(c):
        part = pl.ds(c * piece, piece)
        return remote(
            far_out.at[:, part, :], far_in.at[:, part, :], rf_s.at[c], rf_r.at[c], far_dev, m
        )

    def near_copy(c):
        part = pl.ds(c * piece, piece)
        return remote(
            near_out.at[:, part, :], near_in.at[:, part, :], rn_s.at[c], rn_r.at[c], near_dev, m
        )

    first = slots // 3
    second = slots - slots // 3
    lax.fori_loop(0, first, backward_inner, 0)
    far_out[...] = reduced(0)

    @pl.when(has_far)
    def _():
        for c in range(chunks):
            far_copy(c).start()

    near_out[...] = reduced(1)

    def pass_on(c):
        @pl.when(has_back)
        def _():
            part = pl.ds(c * piece, piece)
            far_copy(c).wait_recv()
            near_out[:, part, :] = near_out[:, part, :] + far_in[:, part, :]

        near_copy(c).start()

    lax.fori_loop(first, second, backward_inner, 0)
    pass_on(0)
    lax.fori_loop(second, slots, backward_inner, 0)
    for j in range(nm - 1):
        reduce_copy(2, j).start()
    for c in range(1, chunks):
        pass_on(c)

    own_sum = reduced(2)
    illum_near().wait_recv()
    weight = 1.0 / (illum[rows_of(1, m), :] + il_near_in[...] + 1.0)
    for c in range(chunks):
        near_copy(c).wait_recv()
        part = slice(c * piece, (c + 1) * piece)
        out_ref[:, part, :] = ext[:, rows_of(1, m, c, piece), :] + (
            own_sum[:, part] + near_in[:, part, :]
        ) * weight[part]

    for c in range(chunks):
        halo(c).wait_send()
        near_copy(c).wait_send()
        for j in range(nm - 1):
            spread(near_blk, c, j, brn_s, brn_r).wait_send()
    for j in range(nm - 1):
        pp_copy(j).wait_send()
        for s in range(slots):
            power_copy(s, j).wait_send()
        for b in range(3):
            reduce_copy(b, j).wait_send()
    illum_near().wait_send()

    @pl.when(has_far)
    def _():
        illum_far().wait_send()
        for c in range(chunks):
            far_copy(c).wait_send()
            for j in range(nm - 1):
                spread(far_blk, c, j, brf_s, brf_r).wait_send()

    @pl.when(has_back)
    def _():
        for c in range(chunks):
            forward_near(c).wait_send()


def local(object_field, probe, measured, row_offsets, col_offsets, tile_counts):
    n, nm = lax.axis_size("pos"), lax.axis_size("mode")
    tile, cols = object_field.shape[1:]
    slots, pat = measured.shape[:2]
    modes = probe.shape[1]
    share = tile // nm
    chunks = min(8, share // 8)
    f32, bf16 = jnp.float32, jnp.bfloat16
    vmem = pl.BlockSpec(memory_space=pltpu.VMEM)
    anywhere = pl.BlockSpec(memory_space=pltpu.HBM)
    dma = pltpu.SemaphoreType.DMA
    others = nm - 1
    scratch = [
        pltpu.SMEM((slots,), jnp.int32),
        pltpu.SMEM((slots,), jnp.int32),
        pltpu.SMEM((1,), jnp.int32),
        pltpu.VMEM((2, modes, pat, pat), f32),
        pltpu.VMEM((slots, pat, pat), f32),
        pltpu.VMEM((2 * pat, 2 * pat), bf16),
        pltpu.VMEM((2 * pat, 2 * pat), bf16),
        dma((6,)),
        pltpu.VMEM((2, pat, pat), f32),
        pltpu.VMEM((slots, 2, 2 * pat, pat), bf16),
        pltpu.VMEM((slots, 2, pat, 2 * pat), bf16),
        pltpu.VMEM((slots, modes, 2 * pat, pat), bf16),
        pltpu.VMEM((slots, 2, modes, pat, pat), f32),
        pltpu.VMEM((slots, modes, 2 * pat, pat), f32),
        pltpu.VMEM((modes * pat, 2 * pat), bf16),
        pltpu.VMEM((modes * tile, 2 * pat), f32),
        pltpu.VMEM((2, 3 * tile, cols), f32),
        pltpu.VMEM((2, 3 * tile, cols), f32),
        pltpu.VMEM((3 * tile, cols), f32),
        pltpu.VMEM((slots, modes, 2, pat, pat), bf16),
        pltpu.VMEM((slots, modes * pat, 2 * pat), f32),
        pltpu.VMEM((slots, pat, pat), f32),
        pltpu.VMEM((slots, others, pat, pat), f32),
        pltpu.VMEM((pat, pat), f32),
        pltpu.VMEM((others, pat, pat), f32),
        pltpu.VMEM((others, 3, 2, share, cols), f32),
        pltpu.VMEM((2, share, cols), f32),
        pltpu.VMEM((2, share, cols), f32),
        pltpu.VMEM((2, share, cols), f32),
        pltpu.VMEM((2, share, cols), f32),
        pltpu.VMEM((share, cols), f32),
        pltpu.VMEM((share, cols), f32),
        pltpu.VMEM((share, cols), f32),
        dma((chunks,)), dma((chunks,)), dma((chunks,)), dma((chunks,)),
        dma((others, chunks)), dma((others, chunks)), dma((others, chunks)), dma((others, chunks)),
        dma((slots, others)), dma((slots, others)), dma((others,)), dma((others,)),
        dma((1,)), dma((1,)), dma((1,)), dma((1,)),
        dma((others, 3)), dma((others, 3)),
        dma((chunks,)), dma((chunks,)), dma((chunks,)), dma((chunks,)),
    ]
    return pl.pallas_call(
        functools.partial(kernel, n, nm, chunks),
        out_shape=pltpu.VMEM((2, share, cols), f32),
        in_specs=[anywhere] * 6,
        out_specs=vmem,
        scratch_shapes=scratch,
        compiler_params=pltpu.CompilerParams(
            collective_id=0, has_side_effects=True, vmem_limit_bytes=65200 * 1024
        ),
    )(
        row_offsets, col_offsets, tile_counts, object_field, probe, measured
    )


def solution(mesh):
    in_specs = (
        P(None, "pos", None),
        P(None, "mode", None, None),
        P("pos", None, None),
        P("pos"),
        P("pos"),
        P("pos"),
    )
    out_specs = P(None, ("pos", "mode"), None)
    return jax.shard_map(local, mesh=mesh, in_specs=in_specs, out_specs=out_specs, check_vma=False)
```

```python
import functools
import math

import jax
import jax.numpy as jnp
from jax import lax
from jax.experimental import pallas as pl
from jax.experimental.pallas import tpu as pltpu
from jax.sharding import PartitionSpec as P

MESH = pl.DeviceIdType.MESH


def sine_of(step, period):
    step = jnp.bitwise_and(step, period - 1)
    step = jnp.where(step >= period // 2, step - period, step)
    step = jnp.where(step > period // 4, period // 2 - step, step)
    step = jnp.where(step < -(period // 4), -(period // 2) - step, step)
    x = step.astype(jnp.float32) * (2.0 * math.pi / period)
    y = x * x
    total = jnp.full_like(x, -1.0 / math.factorial(11))
    for order in (9, 7, 5, 3, 1):
        total = total * y + (-1.0) ** (order // 2) / math.factorial(order)
    return x * total


def dft_tables(pattern):
    rows = lax.broadcasted_iota(jnp.int32, (pattern, pattern), 0)
    columns = lax.broadcasted_iota(jnp.int32, (pattern, pattern), 1)
    phases = rows * columns
    factor = 1.0 / math.sqrt(pattern)
    real = sine_of(phases + pattern // 4, pattern) * factor
    imag = -sine_of(phases, pattern) * factor
    return real, imag


def kernel(
    n, nm, chunks,
    row_hbm, col_hbm, count_hbm, obj_hbm, probe_hbm, meas_hbm,
    out_ref,
    row_ref, col_ref, count_ref, probe_ref, meas_ref, plain_ref, turned_ref, load_s,
    base, left, right, fixed_ref, spun, early, stage, delta_ref, ext, acc, illum, exit_ref, wave_ref, power, power_in, pp, pp_in, red_in,
    far_out, far_in, near_out, near_in, il_far_in, il_near_out, il_near_in,
    halo_s, halo_r, fwd_s, fwd_r, brn_s, brn_r, brf_s, brf_r,
    pow_s, pow_r, pp_s, pp_r, ilf_s, ilf_r, iln_s, iln_r,
    red_s, red_r, rf_s, rf_r, rn_s, rn_r,
):
    tile, cols = obj_hbm.shape[1], obj_hbm.shape[2]
    slots, pat = meas_ref.shape[0], meas_ref.shape[1]
    modes = probe_ref.shape[1]
    share = tile // nm
    piece = share // chunks
    assert pat == 2 * tile
    f32, bf16 = jnp.float32, jnp.bfloat16

    p = lax.axis_index("pos")
    m = lax.axis_index("mode")
    odd = lax.rem(p, 2)
    near_dev = p + 1 - 2 * odd
    far_blk = 2 * odd
    near_blk = 2 - far_blk
    far_raw = p - 2 + 4 * odd
    back_raw = p + 2 - 4 * odd
    has_far = jnp.logical_and(far_raw >= 0, far_raw < n)
    has_back = jnp.logical_and(back_raw >= 0, back_raw < n)
    far_dev = lax.rem(far_raw + n, n)
    back_dev = lax.rem(back_raw + n, n)
    others = [lax.rem(m + j, nm) for j in range(1, nm)]

    def rows_of(block, mode, c=0, size=None):
        size = share if size is None else size
        return pl.ds(pl.multiple_of(block * tile + mode * share + c * piece, 8), size)

    def remote(src, dst, s, r, pos, mode):
        return pltpu.make_async_remote_copy(
            src_ref=src, dst_ref=dst, send_sem=s, recv_sem=r,
            device_id=(pos, mode), device_id_type=MESH,
        )

    own = ext.at[:, tile : 2 * tile, :]
    pairs = (
        (probe_hbm, probe_ref), (row_hbm, row_ref), (col_hbm, col_ref), (count_hbm, count_ref),
        (obj_hbm, own), (meas_hbm, meas_ref),
    )
    loads = [pltpu.make_async_copy(a, b, load_s.at[i]) for i, (a, b) in enumerate(pairs)]
    def fill(table, real, imag, sign):
        high, wide = table.shape[0] // 2, table.shape[1] // 2
        real = real.astype(jnp.bfloat16)
        table[:high, :wide] = real
        table[high:, wide:] = real
        table[:high, wide:] = (sign * imag).astype(jnp.bfloat16)
        table[high:, :wide] = (-sign * imag).astype(jnp.bfloat16)

    barrier = pltpu.get_barrier_semaphore()
    pl.semaphore_signal(barrier, inc=1, device_id=(near_dev, m), device_id_type=MESH)
    for other in others:
        pl.semaphore_signal(barrier, inc=1, device_id=(p, other), device_id_type=MESH)

    @pl.when(has_far)
    def _():
        pl.semaphore_signal(barrier, inc=1, device_id=(far_dev, m), device_id_type=MESH)

    @pl.when(has_back)
    def _():
        pl.semaphore_signal(barrier, inc=1, device_id=(back_dev, m), device_id_type=MESH)

    greeted = has_far.astype(jnp.int32) + has_back.astype(jnp.int32)
    for load in loads:
        load.start()
    real, imag = dft_tables(pat)
    base[0] = real
    base[1] = imag
    for table, sign in ((plain_ref, -1.0), (turned_ref, 1.0)):
        fill(table, real, imag, sign)
    loads[0].wait()
    total = jnp.zeros((pat, pat), jnp.float32)
    for k in range(modes):
        total = total + probe_ref[0, k] * probe_ref[0, k] + probe_ref[1, k] * probe_ref[1, k]
    pp[...] = total
    for load in loads[1:]:
        load.wait()
    pl.semaphore_wait(barrier, nm + greeted)

    def halo(c):
        return remote(
            obj_hbm.at[:, rows_of(0, m, c, piece), :], ext.at[:, rows_of(far_blk, m, c, piece), :],
            halo_s.at[c], halo_r.at[c], near_dev, m,
        )

    def forward_near(c):
        return remote(
            ext.at[:, rows_of(near_blk, m, c, piece), :],
            ext.at[:, rows_of(far_blk, m, c, piece), :],
            fwd_s.at[c], fwd_r.at[c], back_dev, m,
        )

    def spread(block, c, j, s, r):
        where = rows_of(block, m, c, piece)
        return remote(
            ext.at[:, where, :], ext.at[:, where, :], s.at[j, c], r.at[j, c], p, others[j]
        )

    for c in range(chunks):
        halo(c).start()

    def pp_copy(j):
        return remote(pp, pp_in.at[j], pp_s.at[j], pp_r.at[j], p, others[j])

    for j in range(nm - 1):
        pp_copy(j).start()

    acc[...] = jnp.zeros_like(acc)
    illum[...] = jnp.zeros_like(illum)

    @pl.when(jnp.logical_not(has_far))
    def _():
        ext[:, pl.ds(pl.multiple_of(far_blk * tile, 8), tile), :] = jnp.zeros(
            (2, tile, cols), jnp.float32
        )

    line = lax.broadcasted_iota(jnp.int32, (tile, cols), 0)

    def narrowed(rows, slot):
        return pltpu.roll(rows, lax.rem(cols - col_ref[slot], cols), 1)[:, :pat]

    def widened(values, slot):
        blank = jnp.zeros((tile, cols - pat), f32)
        return pltpu.roll(jnp.concatenate([values, blank], axis=1), col_ref[slot], 1)

    def add_outer(total, values, slot):
        wide, below = widened(values, slot), line < row_ref[slot]
        total[:tile, :] += jnp.where(below, 0.0, wide)
        total[2 * tile :, :] += jnp.where(below, wide, 0.0)

    def add_inner(total, values, slot):
        total[tile : 2 * tile, :] += widened(values, slot)

    def exits(s, k, part, win_re, win_im):
        rows = slice(part * tile, (part + 1) * tile)
        probe_re, probe_im = spun[s, 0, k, rows, :], spun[s, 1, k, rows, :]
        exit_re = (probe_re * win_re - probe_im * win_im).astype(bf16)
        exit_im = (probe_re * win_im + probe_im * win_re).astype(bf16)
        stacked = jnp.concatenate([exit_re, exit_im], axis=0)
        exit_ref[s, k, part] = stacked
        return jnp.dot(left[s, part], stacked, preferred_element_type=f32)

    def turn_tables(s):
        shift = row_ref[s]
        real, imag = (pltpu.roll(base[i], shift, 1) for i in (0, 1))
        for part in (0, 1):
            columns = slice(part * tile, (part + 1) * tile)
            fill(left.at[s, part], real[:, columns], imag[:, columns], -1.0)
        real, imag = (pltpu.roll(base[i], shift, 0) for i in (0, 1))
        for part in (0, 1):
            rows = slice(part * tile, (part + 1) * tile)
            fill(right.at[s, part], real[rows], imag[rows], 1.0)

    def turn_probes(s):
        for i in (0, 1):
            for k in range(modes):
                spun[s, i, k] = pltpu.roll(probe_ref[i, k], row_ref[s], 0)

    def start_products(s):
        win_re = narrowed(ext[0, tile : 2 * tile, :], s)
        win_im = narrowed(ext[1, tile : 2 * tile, :], s)
        for k in range(modes):
            early[s, k] = exits(s, k, 1, win_re, win_im)

    work = [
        functools.partial(do, s)
        for s in range(slots)
        for do in (turn_tables, turn_probes, start_products)
    ]

    for c in range(max(chunks, len(work))):
        if c < len(work):
            work[c]()
        if c >= chunks:
            continue
        halo(c).wait_recv()

        @pl.when(has_back)
        def _():
            forward_near(c).start()

        for j in range(nm - 1):
            spread(near_blk, c, j, brn_s, brn_r).start()

    for j in range(nm - 1):
        pp_copy(j).wait_recv()

    live = count_ref[0]

    def add_illum(s, carry):
        whole = pp[...]
        for j in range(nm - 1):
            whole = whole + pp_in[j]
        whole = jnp.where(s < live, whole, 0.0)
        whole = pltpu.roll(whole, row_ref[s], 0)
        add_outer(illum, whole[:tile], s)
        add_inner(illum, whole[tile:], s)
        return carry

    def relay(c):
        @pl.when(has_far)
        def _():
            forward_near(c).wait_recv()
            for j in range(nm - 1):
                spread(far_blk, c, j, brf_s, brf_r).start()

    for c in range(chunks):
        relay(c)
    lax.fori_loop(0, slots, add_illum, 0)

    def illum_far():
        return remote(
            illum.at[rows_of(far_blk, m), :], il_far_in, ilf_s.at[0], ilf_r.at[0], far_dev, m
        )

    def illum_near():
        return remote(il_near_out, il_near_in, iln_s.at[0], iln_r.at[0], near_dev, m)

    @pl.when(has_far)
    def _():
        illum_far().start()

    for c in range(chunks):
        for j in range(nm - 1):
            spread(near_blk, c, j, brn_s, brn_r).wait_recv()

    @pl.when(has_far)
    def _():
        for c in range(chunks):
            for j in range(nm - 1):
                spread(far_blk, c, j, brf_s, brf_r).wait_recv()

    def power_copy(s, j):
        return remote(
            power.at[s], power_in.at[s, j], pow_s.at[s, j], pow_r.at[s, j], p, others[j]
        )

    def forward(s, carry):
        below = line < row_ref[s]
        win_re, win_im = (
            narrowed(jnp.where(below, ext[i, 2 * tile :, :], ext[i, :tile, :]), s) for i in (0, 1)
        )
        for k in range(modes):
            half = early[s, k] + exits(s, k, 0, win_re, win_im)
            half = half.astype(bf16)
            stage[k * pat : (k + 1) * pat, :pat] = half[:pat]
            stage[k * pat : (k + 1) * pat, pat:] = half[pat:]
        wave_ref[s] = jnp.dot(stage[...], turned_ref[...], preferred_element_type=f32)
        model = jnp.zeros((pat, pat), f32)
        for k in range(modes):
            wave = wave_ref[s, k * pat : (k + 1) * pat, :]
            model = model + wave[:, :pat] * wave[:, :pat] + wave[:, pat:] * wave[:, pat:]
        power[s] = model
        for j in range(nm - 1):
            power_copy(s, j).start()
        return carry

    lax.fori_loop(0, slots, forward, 0)

    @pl.when(has_back)
    def _():
        illum_far().wait_recv()
        il_near_out[...] = illum[rows_of(near_blk, m), :] + il_far_in[...]

    @pl.when(jnp.logical_not(has_back))
    def _():
        il_near_out[...] = illum[rows_of(near_blk, m), :]

    illum_near().start()

    def numerators(s, part):
        for k in range(modes):
            back = jnp.dot(right[s, part], fixed_ref[s, k], preferred_element_type=f32)
            back = back.astype(bf16)
            stage[k * tile : (k + 1) * tile, :pat] = back[:tile]
            stage[k * tile : (k + 1) * tile, pat:] = back[tile:]
        delta_ref[...] = jnp.dot(
            stage[: modes * tile, :], plain_ref[...], preferred_element_type=f32
        )
        numer_re = jnp.zeros((tile, pat), f32)
        numer_im = jnp.zeros((tile, pat), f32)
        rows = slice(part * tile, (part + 1) * tile)
        for k in range(modes):
            delta = delta_ref[k * tile : (k + 1) * tile, :]
            delta_re = delta[:, :pat] - exit_ref[s, k, part, :tile, :].astype(f32)
            delta_im = delta[:, pat:] - exit_ref[s, k, part, tile:, :].astype(f32)
            probe_re, probe_im = spun[s, 0, k, rows, :], spun[s, 1, k, rows, :]
            numer_re = numer_re + probe_re * delta_re + probe_im * delta_im
            numer_im = numer_im + probe_re * delta_im - probe_im * delta_re
        on = s < live
        return jnp.where(on, numer_re, 0.0), jnp.where(on, numer_im, 0.0)

    def backward_outer(s, carry):
        model = power[s]
        for j in range(nm - 1):
            power_copy(s, j).wait_recv()
            model = model + power_in[s, j]
        scaling = jnp.sqrt(meas_ref[s]) / jnp.maximum(jnp.sqrt(model), 1.0)
        for k in range(modes):
            block = slice(k * pat, (k + 1) * pat)
            fixed_ref[s, k, :pat, :] = (scaling * wave_ref[s, block, :pat]).astype(bf16)
            fixed_ref[s, k, pat:, :] = (scaling * wave_ref[s, block, pat:]).astype(bf16)
        for i, numer in enumerate(numerators(s, 0)):
            add_outer(acc.at[i], numer, s)
        return carry

    def backward_inner(s, carry):
        for i, numer in enumerate(numerators(s, 1)):
            add_inner(acc.at[i], numer, s)
        return carry

    lax.fori_loop(0, slots, backward_outer, 0)

    blocks = (far_blk, near_blk, 1)

    def reduce_copy(b, j):
        return remote(
            acc.at[:, rows_of(blocks[b], others[j]), :], red_in.at[j, b],
            red_s.at[j, b], red_r.at[j, b], p, others[j],
        )

    for b in (0, 1):
        for j in range(nm - 1):
            reduce_copy(b, j).start()

    def reduced(b):
        value = acc[:, rows_of(blocks[b], m), :]
        for j in range(nm - 1):
            reduce_copy(b, j).wait_recv()
            value = value + red_in[j, b]
        return value

    def far_copy(c):
        part = pl.ds(c * piece, piece)
        return remote(
            far_out.at[:, part, :], far_in.at[:, part, :], rf_s.at[c], rf_r.at[c], far_dev, m
        )

    def near_copy(c):
        part = pl.ds(c * piece, piece)
        return remote(
            near_out.at[:, part, :], near_in.at[:, part, :], rn_s.at[c], rn_r.at[c], near_dev, m
        )

    first = slots // 3
    second = slots - slots // 3
    lax.fori_loop(0, first, backward_inner, 0)
    far_out[...] = reduced(0)

    @pl.when(has_far)
    def _():
        for c in range(chunks):
            far_copy(c).start()

    near_out[...] = reduced(1)

    def pass_on(c):
        @pl.when(has_back)
        def _():
            part = pl.ds(c * piece, piece)
            far_copy(c).wait_recv()
            near_out[:, part, :] = near_out[:, part, :] + far_in[:, part, :]

        near_copy(c).start()

    lax.fori_loop(first, second, backward_inner, 0)
    pass_on(0)
    lax.fori_loop(second, slots, backward_inner, 0)
    for j in range(nm - 1):
        reduce_copy(2, j).start()
    for c in range(1, chunks):
        pass_on(c)

    own_sum = reduced(2)
    illum_near().wait_recv()
    weight = 1.0 / (illum[rows_of(1, m), :] + il_near_in[...] + 1.0)
    for c in range(chunks):
        near_copy(c).wait_recv()
        part = slice(c * piece, (c + 1) * piece)
        out_ref[:, part, :] = ext[:, rows_of(1, m, c, piece), :] + (
            own_sum[:, part] + near_in[:, part, :]
        ) * weight[part]

    for c in range(chunks):
        halo(c).wait_send()
        near_copy(c).wait_send()
        for j in range(nm - 1):
            spread(near_blk, c, j, brn_s, brn_r).wait_send()
    for j in range(nm - 1):
        pp_copy(j).wait_send()
        for s in range(slots):
            power_copy(s, j).wait_send()
        for b in range(3):
            reduce_copy(b, j).wait_send()
    illum_near().wait_send()

    @pl.when(has_far)
    def _():
        illum_far().wait_send()
        for c in range(chunks):
            far_copy(c).wait_send()
            for j in range(nm - 1):
                spread(far_blk, c, j, brf_s, brf_r).wait_send()

    @pl.when(has_back)
    def _():
        for c in range(chunks):
            forward_near(c).wait_send()


def local(object_field, probe, measured, row_offsets, col_offsets, tile_counts):
    n, nm = lax.axis_size("pos"), lax.axis_size("mode")
    tile, cols = object_field.shape[1:]
    slots, pat = measured.shape[:2]
    modes = probe.shape[1]
    share = tile // nm
    chunks = min(8, share // 8)
    f32, bf16 = jnp.float32, jnp.bfloat16
    vmem = pl.BlockSpec(memory_space=pltpu.VMEM)
    anywhere = pl.BlockSpec(memory_space=pltpu.HBM)
    dma = pltpu.SemaphoreType.DMA
    others = nm - 1
    scratch = [
        pltpu.SMEM((slots,), jnp.int32),
        pltpu.SMEM((slots,), jnp.int32),
        pltpu.SMEM((1,), jnp.int32),
        pltpu.VMEM((2, modes, pat, pat), f32),
        pltpu.VMEM((slots, pat, pat), f32),
        pltpu.VMEM((2 * pat, 2 * pat), bf16),
        pltpu.VMEM((2 * pat, 2 * pat), bf16),
        dma((6,)),
        pltpu.VMEM((2, pat, pat), f32),
        pltpu.VMEM((slots, 2, 2 * pat, pat), bf16),
        pltpu.VMEM((slots, 2, pat, 2 * pat), bf16),
        pltpu.VMEM((slots, modes, 2 * pat, pat), bf16),
        pltpu.VMEM((slots, 2, modes, pat, pat), f32),
        pltpu.VMEM((slots, modes, 2 * pat, pat), f32),
        pltpu.VMEM((modes * pat, 2 * pat), bf16),
        pltpu.VMEM((modes * tile, 2 * pat), f32),
        pltpu.VMEM((2, 3 * tile, cols), f32),
        pltpu.VMEM((2, 3 * tile, cols), f32),
        pltpu.VMEM((3 * tile, cols), f32),
        pltpu.VMEM((slots, modes, 2, pat, pat), bf16),
        pltpu.VMEM((slots, modes * pat, 2 * pat), f32),
        pltpu.VMEM((slots, pat, pat), f32),
        pltpu.VMEM((slots, others, pat, pat), f32),
        pltpu.VMEM((pat, pat), f32),
        pltpu.VMEM((others, pat, pat), f32),
        pltpu.VMEM((others, 3, 2, share, cols), f32),
        pltpu.VMEM((2, share, cols), f32),
        pltpu.VMEM((2, share, cols), f32),
        pltpu.VMEM((2, share, cols), f32),
        pltpu.VMEM((2, share, cols), f32),
        pltpu.VMEM((share, cols), f32),
        pltpu.VMEM((share, cols), f32),
        pltpu.VMEM((share, cols), f32),
        dma((chunks,)), dma((chunks,)), dma((chunks,)), dma((chunks,)),
        dma((others, chunks)), dma((others, chunks)), dma((others, chunks)), dma((others, chunks)),
        dma((slots, others)), dma((slots, others)), dma((others,)), dma((others,)),
        dma((1,)), dma((1,)), dma((1,)), dma((1,)),
        dma((others, 3)), dma((others, 3)),
        dma((chunks,)), dma((chunks,)), dma((chunks,)), dma((chunks,)),
    ]
    return pl.pallas_call(
        functools.partial(kernel, n, nm, chunks),
        out_shape=pltpu.VMEM((2, share, cols), f32),
        in_specs=[anywhere] * 6,
        out_specs=vmem,
        scratch_shapes=scratch,
        compiler_params=pltpu.CompilerParams(
            collective_id=0, has_side_effects=True, vmem_limit_bytes=65200 * 1024
        ),
    )(
        row_offsets, col_offsets, tile_counts, object_field, probe, measured
    )


def solution(mesh):
    in_specs = (
        P(None, "pos", None),
        P(None, "mode", None, None),
        P("pos", None, None),
        P("pos"),
        P("pos"),
        P("pos"),
    )
    out_specs = P(None, ("pos", "mode"), None)
    return jax.shard_map(local, mesh=mesh, in_specs=in_specs, out_specs=out_specs, check_vma=False)
```
